128 devices in a mesh: dp: 16 (over x, z_lo, core), owner: 8 (over y, z_hi).
Axes of the slice: x: 4, y: 4, z: 4 (z_hi: 2, z_lo: 2; z = z_hi * 2 + z_lo), core: 2. Of those that a mesh axis runs over, the one named last changes fastest.
Arguments:
- layer_inputs: bfloat16 [16384, 5120], P(('dp', 'owner')), may hold values from -200 to 200
- output_grads: bfloat16 [16384, 13824], P(('dp', 'owner')), may hold values from -200 to 200
- weight_grad: bfloat16 [5120, 13824], P('dp', 'owner'), may hold values from -0.15625 to 0.15625
Outputs:
- preconditioned: bfloat16 [5120, 13824], P('dp')
The draws below stay inside these ranges and needn't reach their ends.
All inputs are finite; a program needn't handle non-finite values.
Results may differ from the reference program's by a relative error of at most 0.017.
Values may be sent and summed in bfloat16 or wider, within the bound.
No kernel may reach another device: no remote copies, remote signals or barrier semaphores. Data moves between devices by JAX's collectives and lax.ppermute only.
A program may use at most 128 MiB of HBM per device.

```python
import math
import jax
import jax.numpy as jnp
from jax import lax

D = 5120
F = 13824
TOK_DEV = 128
BA = 320
BG = 864
TOKENS = 16384


def structure(key, latent, size, low, high):
    row_count, count, rank = latent.shape
    column_count = count * size
    key_coef, key_scale, key_noise, key_order = jax.random.split(key, 4)
    position = jnp.arange(size)
    mixed = jnp.zeros((row_count, count, size), jnp.float32)
    for term in range(3):
        picked = (position + term) % rank
        coef = jax.random.uniform(jax.random.fold_in(key_coef, term), (count, size), jnp.float32, -1.0, 1.0)
        mixed = mixed + jnp.take(latent, picked, axis=2) * coef
    mixed = mixed.reshape(row_count, column_count)
    scale = jnp.exp(jax.random.uniform(key_scale, (column_count,), jnp.float32, math.log(low), math.log(high)))
    block_count = row_count // TOK_DEV
    order = jax.random.permutation(key_order, block_count)
    row_target = order[jnp.arange(row_count) // TOK_DEV]
    column_group = jnp.arange(column_count) * block_count // column_count
    noise_weight = jnp.where(row_target[:, None] == column_group[None, :], 6.0, 0.0)
    noise = jnp.clip(jax.random.normal(key_noise, (row_count, column_count), jnp.float32), -4.0, 4.0)
    return mixed * scale + noise * noise_weight


def draw_layer_inputs(key, part):
    key = jax.random.fold_in(key, 11)
    key_base, key_mix = jax.random.split(key)
    rank = max(BA // 8, 1)
    latent = jnp.clip(0.7 * jax.random.normal(key_base, (TOKENS, D // BA, rank), jnp.float32), -1.7, 1.7)
    return structure(key_mix, latent, BA, 4.0, 30.0).astype(jnp.bfloat16)


def draw_output_grads(key, part):
    key = jax.random.fold_in(key, 23)
    key_base, key_mix = jax.random.split(key)
    rank = max(BG // 8, 1)
    latent = jnp.clip(0.7 * jax.random.normal(key_base, (TOKENS, F // BG, rank), jnp.float32), -1.7, 1.7)
    return structure(key_mix, latent, BG, 4.0, 30.0).astype(jnp.bfloat16)


def block_scale(own_key, shape, shards, low, high):
    def one(axis_at, parts):
        steps = jax.random.uniform(jax.random.fold_in(jax.random.fold_in(own_key, 6), axis_at), (parts,), jnp.float32, low / len(shards), high / len(shards))
        return jnp.repeat(jnp.exp(steps), shape[axis_at] // parts).reshape((-1,) + (1,) * (len(shape) - axis_at - 1))

    factor_of = one(*shards[0])
    for cut in shards[1:]:
        factor_of = factor_of * one(*cut)
    return factor_of


def gaussian(rng, dims, width, most, pieces=(), held_as=jnp.bfloat16):
    level = block_scale(rng, dims, pieces, -0.22, 0.18) if pieces else 1.0
    drawn = jax.random.normal(rng, dims, jnp.float32) * width * level
    return jnp.minimum(jnp.maximum(drawn, -most), most).astype(held_as)


def setup_inputs(seed: int = 0) -> dict:
    streams_of = jax.random.split(jax.random.key(seed), 4)
    return {
        "layer_inputs": draw_layer_inputs(jax.random.fold_in(streams_of[3], 71), 0),
        "output_grads": draw_output_grads(jax.random.fold_in(streams_of[3], 71), 0),
        "weight_grad": gaussian(streams_of[2], (D, F), 0.01, 0.15625, ((0, 16), (1, 8))),
    }


damping = 0.1

def gram_blocks(rows, size):
    count = rows.shape[1] // size
    stacked = jnp.transpose(rows.reshape(rows.shape[0], count, size), (1, 0, 2))
    return lax.map(lambda piece: jnp.dot(piece.T.astype(jnp.float32), piece.astype(jnp.float32), preferred_element_type=jnp.float32), stacked)

def damped_inverse(factor):
    size = factor.shape[-1]
    identity = jnp.eye(size, dtype=jnp.float32)
    lower = jnp.linalg.cholesky(factor + damping * identity)
    target = jnp.broadcast_to(identity, factor.shape)
    return jax.scipy.linalg.cho_solve((lower, True), target).astype(jnp.bfloat16)

def reference(layer_inputs, output_grads, weight_grad):
    act_factor = gram_blocks(layer_inputs, BA) / TOKENS
    grad_factor = gram_blocks(output_grads, BG) / TOKENS
    act_inverse = damped_inverse(act_factor)
    grad_inverse = damped_inverse(grad_factor)
    stacked = weight_grad.reshape(D // BA, BA, F)
    left = lax.map(lambda pair: jnp.dot(pair[0].astype(jnp.float32), pair[1].astype(jnp.float32), preferred_element_type=jnp.float32).astype(jnp.bfloat16), (act_inverse, stacked))
    left = left.reshape(D, F)
    columns = jnp.transpose(left.reshape(D, F // BG, BG), (1, 0, 2))
    right = lax.map(lambda pair: jnp.dot(pair[0].astype(jnp.float32), pair[1].astype(jnp.float32), preferred_element_type=jnp.float32).astype(jnp.bfloat16), (columns, grad_inverse))
    return jnp.transpose(right, (1, 0, 2)).reshape(D, F)
```

```python
import functools
import jax, jax.numpy as jnp
from jax import lax
from jax.experimental import pallas as pl
from jax.experimental.pallas import tpu as pltpu
f32=jnp.float32; bf16=jnp.bfloat16
NB=128

def split3(x):
    h=x.astype(bf16); r=x-h.astype(f32)
    m=r.astype(bf16); l=(r-m.astype(f32)).astype(bf16)
    return h,m,l

def bc(x,j):
    return jnp.broadcast_to(x[j:j+1,:],(8,128))

def eliminate(chains):
    lane=lax.broadcasted_iota(jnp.int32,(8,128),1); sub=lax.broadcasted_iota(jnp.int32,(8,128),0)
    outs=[[] for _ in chains]
    for g in range(16):
        lo=8*g
        ing=(lane>=lo)&(lane<lo+8)
        eye=jnp.where(lane-lo==sub,1.0,0.0).astype(f32)
        st=[]
        for rows in chains:
            R=rows[g]
            B=[jnp.broadcast_to(R[:,lo+j:lo+j+1],(8,128)) for j in range(8)]
            st.append([jnp.where(ing,eye,R),B,jnp.zeros((8,128),f32)])
        for j in range(8):
            for s_ in st:
                R,B,U=s_
                p=bc(B[j],j)
                rs=lax.rsqrt(p)
                rs=rs*(1.5-0.5*p*rs*rs)
                inv=rs*rs
                m=bc(R,j)*inv
                U=jnp.where(sub==j,R*rs,U)
                R=jnp.where(sub==j,m,R-B[j]*m)
                for q in range(j+1,8):
                    s=bc(B[q],j)*inv
                    B[q]=jnp.where(sub==j,s,B[q]-B[j]*s)
                s_[0]=R; s_[2]=U
        for ci,(rows,s_) in enumerate(zip(chains,st)):
            W=s_[0]; outs[ci].append(s_[2])
            w=[bc(W,j) for j in range(8)]
            for i in range(g+1,16):
                a=rows[i]
                acc=jnp.where(ing,0.0,a)
                for j in range(8):
                    acc=acc-jnp.broadcast_to(a[:,lo+j:lo+j+1],(8,128))*w[j]
                rows[i]=acc
    return outs

def dot(a,b,ca,cb):
    return lax.dot_general(a,b,(((ca,),(cb,)),((),())),preferred_element_type=f32)

def load_diag(M,k):
    cols=pl.ds(pl.multiple_of(k*NB,NB),NB)
    return [M[pl.ds(pl.multiple_of(k*NB+8*i,8),8),cols] for i in range(16)]

def store_lower(LD,rows):
    lane=lax.broadcasted_iota(jnp.int32,(8,128),1); sub=lax.broadcasted_iota(jnp.int32,(8,128),0)
    for i,u in enumerate(rows):
        LD[8*i:8*i+8,:]=jnp.where(lane<=sub+8*i,u,0.0)

def panel(M,LD,k,n):
    nb=n//NB; r0=k*NB
    M[r0:r0+NB,r0:r0+NB]=jnp.where(lax.broadcasted_iota(jnp.int32,(NB,NB),0)==lax.broadcasted_iota(jnp.int32,(NB,NB),1),1.0,0.0).astype(f32)
    lh,lm,ll=split3(LD[...])
    mh,mm,ml=split3(M[r0:r0+NB,:])
    hm=jnp.concatenate([mh,mm],0); lhh=jnp.concatenate([ml,mh],0)
    U=dot(jnp.concatenate([lh,lh],1),hm,1,0)+dot(jnp.concatenate([lm,lm],1),hm,1,0)+dot(jnp.concatenate([lh,ll],1),lhh,1,0)
    M[r0:r0+NB,:]=U
    if k+1<nb:
        h,m,l=split3(U)
        c=r0+NB
        hm=jnp.concatenate([h,m],0); lhh=jnp.concatenate([l,h],0)
        ht,mt,lt=h[:,c:].T,m[:,c:].T,l[:,c:].T
        S=dot(jnp.concatenate([ht,ht],1),hm,1,0)+dot(jnp.concatenate([mt,mt],1),hm,1,0)+dot(jnp.concatenate([ht,lt],1),lhh,1,0)
        M[c:,r0:r0+NB]=jnp.zeros((n-c,NB),f32)
        M[c:,:]=M[c:,:]-S

def steps(M,LD,n,Ma,LDa,na,k0,k1):
    both=min(k1,na//NB) if Ma is not None else k0
    def body2(k,_):
        g,a=eliminate([load_diag(M,k),load_diag(Ma,k)])
        store_lower(LD,g); store_lower(LDa,a)
        for kk in range(k0,both):
            @pl.when(k==kk)
            def _():
                panel(M,LD,kk,n); panel(Ma,LDa,kk,na)
        return 0
    def body1(k,_):
        g,=eliminate([load_diag(M,k)])
        store_lower(LD,g)
        for kk in range(max(k0,both),k1):
            @pl.when(k==kk)
            def _(): panel(M,LD,kk,n)
        return 0
    if both>k0: lax.fori_loop(k0,both,body2,0)
    if k1>max(k0,both): lax.fori_loop(max(k0,both),k1,body1,0)


import itertools
import math
import numpy as np
from jax.sharding import Mesh, PartitionSpec as P

BA = 320
BG = 864
GP = 896
AP = 384
WIDE = BG + BA
DAMPING = 0.1
SIZES = dict(x=4, zl=2, c=2, y=4, zh=2)
GB = [(i, j) for i in range(GP // NB) for j in range(i, GP // NB)]
AB = [(i, j) for i in range(AP // NB) for j in range(i, AP // NB)]
ROWS = (len(GB) + len(AB)) * NB
CHUNK = ROWS // 8
VMEM = pltpu.CompilerParams(vmem_limit_bytes=56 << 20)


def move(a, names, target):
    dims = [SIZES[n] for n in names]
    pairs = []
    for at in itertools.product(*map(range, dims)):
        to = target(*at)
        pairs.append((int(np.ravel_multi_index(at, dims)), int(np.ravel_multi_index(to, dims))))
    return lax.ppermute(a, names, pairs)


def along_z(a, d):
    def target(zl, zh):
        z = (2 * zh + zl + d) % 4
        return z % 2, z // 2
    return move(a, ("zl", "zh"), target)


def along_y(a, d):
    return move(a, ("y",), lambda y: ((y + d) % 4,))


def swap_core(a):
    return move(a, ("c",), lambda c: (1 - c,))


def swap_zh(a):
    return move(a, ("zh",), lambda h: (1 - h,))


def in_plane(a, d, first):
    def target(x, c, y):
        return ((x + d) % 4, c, y) if (c == 0) == first else (x, c, (y + d) % 4)
    return move(a, ("x", "c", "y"), target)


def turn_kernel(g_ref, x_ref, o_ref):
    def put(ref, size, base):
        for t in range(ref.shape[1] // NB):
            tile = ref[:, t * NB:(t + 1) * NB].T
            at, end = t * NB, (t + 1) * NB
            while at < end:
                b = at // size
                stop = min(end, (b + 1) * size)
                o_ref[b, base + at - b * size:base + stop - b * size, :] = tile[at - t * NB:stop - t * NB, :]
                at = stop
    put(g_ref, BG, 0)
    put(x_ref, BA, BG)


def turn(g, x):
    return pl.pallas_call(
        turn_kernel,
        out_shape=jax.ShapeDtypeStruct((16, WIDE, NB), bf16),
        compiler_params=VMEM,
    )(g, x)


def gram_kernel(at_ref, t_ref, mine_ref, other_ref, g_ref, a_ref, p_ref):
    z, c = at_ref[0], at_ref[1]
    g_ref[BG:, :] = jnp.zeros((GP - BG, 16 * NB), bf16)
    a_ref[BA:, :] = jnp.zeros((AP - BA, 16 * NB), bf16)
    for s in range(16):
        g_ref[:BG, s * NB:(s + 1) * NB] = t_ref[s, :BG, :]
        a_ref[:BA, s * NB:(s + 1) * NB] = t_ref[s, BG:, :]

    def products(ref, n, blocks, base):
        for r0 in range(0, n, 2 * NB):
            rows = min(2 * NB, n - r0)
            d = dot(ref[r0:r0 + rows, :], ref[r0:, :], 1, 1)
            for k, (i, j) in enumerate(blocks):
                if r0 <= i * NB < r0 + rows:
                    p_ref[base + k * NB:base + (k + 1) * NB, :] = d[i * NB - r0:(i + 1) * NB - r0, j * NB - r0:(j + 1) * NB - r0]

    products(g_ref, GP, GB, 0)
    products(a_ref, AP, AB, len(GB) * NB)
    for q in range(4):
        d = lax.rem(q - z + 4, 4)
        rows = pl.ds(pl.multiple_of(d * CHUNK, 8), CHUNK)
        first, second = p_ref[q * CHUNK:(q + 1) * CHUNK, :], p_ref[(4 + q) * CHUNK:(5 + q) * CHUNK, :]
        mine_ref[rows, :] = jnp.where(c == 0, first, second)
        other_ref[rows, :] = jnp.where(c == 0, second, first)


def gram(at, t):
    half = jax.ShapeDtypeStruct((4 * CHUNK, NB), f32)
    return pl.pallas_call(
        gram_kernel,
        out_shape=(half, half),
        in_specs=[pl.BlockSpec(memory_space=pltpu.SMEM), pl.BlockSpec(memory_space=pltpu.VMEM)],
        scratch_shapes=[
            pltpu.VMEM((GP, 16 * NB), bf16),
            pltpu.VMEM((AP, 16 * NB), bf16),
            pltpu.VMEM((ROWS, NB), f32),
        ],
        compiler_params=VMEM,
    )(at, t)


def sum_over_copies(mine, other):
    h = mine + swap_core(other)
    part = [h[d * CHUNK:(d + 1) * CHUNK] for d in range(4)]
    got = [along_z(part[d], d) for d in (1, 2, 3)]
    s = part[0] + got[0] + got[1] + got[2]
    own = jnp.concatenate([s] + [along_z(s, d) for d in (1, 2, 3)], axis=0)
    return own, swap_core(own)


def eye(n):
    return jnp.where(
        lax.broadcasted_iota(jnp.int32, (n, n), 0) == lax.broadcasted_iota(jnp.int32, (n, n), 1), 1.0, 0.0
    ).astype(f32)


def first_kernel(at_ref, own_ref, part_ref, m_ref, t_ref, inv_ref, p_ref, LD, Ma, LDa):
    z, c = at_ref[0], at_ref[1]
    for d in range(4):
        q = lax.rem(z - d + 4, 4)
        p_ref[pl.ds(pl.multiple_of((4 * c + q) * CHUNK, 8), CHUNK), :] = own_ref[d * CHUNK:(d + 1) * CHUNK, :]
        p_ref[pl.ds(pl.multiple_of((4 * (1 - c) + q) * CHUNK, 8), CHUNK), :] = part_ref[d * CHUNK:(d + 1) * CHUNK, :]
    tokens = 16384.0

    def unpack(M, n, blocks, base):
        M[...] = jnp.zeros((n, n), f32)
        for k, (i, j) in enumerate(blocks):
            block = p_ref[base + k * NB:base + (k + 1) * NB, :] / tokens
            if i == j:
                block = block + DAMPING * eye(NB)
            M[i * NB:(i + 1) * NB, j * NB:(j + 1) * NB] = block

    unpack(m_ref, GP, GB, 0)
    unpack(Ma, AP, AB, len(GB) * NB)
    steps(m_ref, LD, GP, Ma, LDa, AP, 0, 4)
    rows = pl.ds(pl.multiple_of(c * NB, NB), NB)
    t_ref[:, :256] = m_ref[rows, :256].astype(bf16)
    t_ref[:, 256:] = m_ref[pl.ds(pl.multiple_of(256 + c * NB, NB), NB), :512].astype(bf16)
    keep = lax.broadcasted_iota(jnp.int32, (NB, NB), 0) >= lax.broadcasted_iota(jnp.int32, (NB, NB), 1)
    @pl.when(c == 0)
    def _():
        t_ref[:, 0:128] = jnp.where(keep, t_ref[:, 0:128], 0)
        t_ref[:, 128:256] = jnp.zeros((NB, NB), bf16)
        t_ref[:, 512:640] = jnp.where(keep, t_ref[:, 512:640], 0)
        t_ref[:, 640:768] = jnp.zeros((NB, NB), bf16)

    @pl.when(c == 1)
    def _():
        t_ref[:, 128:256] = jnp.where(keep, t_ref[:, 128:256], 0)
        t_ref[:, 640:768] = jnp.where(keep, t_ref[:, 640:768], 0)

    n = AP // NB
    for i in range(n):
        Ma[i * NB:(i + 1) * NB, i * NB:(i + 1) * NB] = jnp.where(keep, Ma[i * NB:(i + 1) * NB, i * NB:(i + 1) * NB], 0.0)
        for j in range(i + 1, n):
            Ma[i * NB:(i + 1) * NB, j * NB:(j + 1) * NB] = jnp.zeros((NB, NB), f32)
    L = Ma[:BA, :BA]
    inv_ref[...] = lax.dot_general(
        L, L, (((0,), (0,)), ((), ())), precision=lax.Precision.HIGHEST, preferred_element_type=f32
    ).astype(bf16)


def first_inverse(at, own, part):
    return pl.pallas_call(
        first_kernel,
        out_shape=(
            jax.ShapeDtypeStruct((GP, GP), f32),
            jax.ShapeDtypeStruct((NB, 768), bf16),
            jax.ShapeDtypeStruct((BA, BA), bf16),
        ),
        in_specs=[pl.BlockSpec(memory_space=pltpu.SMEM)] + [pl.BlockSpec(memory_space=pltpu.VMEM)] * 2,
        scratch_shapes=[
            pltpu.VMEM((ROWS, NB), f32),
            pltpu.VMEM((NB, NB), f32),
            pltpu.VMEM((AP, AP), f32),
            pltpu.VMEM((NB, NB), f32),
        ],
        compiler_params=VMEM,
    )(at, own, part)


def second_kernel(at_ref, m_in, t_ref, M, LD, s_ref):
    c = at_ref[1]
    M[...] = m_in[...]
    steps(M, LD, GP, None, None, 0, 4, 7)
    keep = lax.broadcasted_iota(jnp.int32, (NB, NB), 0) >= lax.broadcasted_iota(jnp.int32, (NB, NB), 1)

    def diag(i):
        return jnp.where(keep, M[i * NB:(i + 1) * NB, i * NB:(i + 1) * NB], 0.0).astype(bf16)

    s_ref[:256, :512] = M[512:768, :512].astype(bf16)
    s_ref[:NB, 512:640] = diag(4)
    s_ref[:NB, 640:768] = jnp.zeros((NB, NB), bf16)
    s_ref[NB:256, 512:640] = M[640:768, 512:640].astype(bf16)
    s_ref[NB:256, 640:768] = diag(5)
    s_ref[256:352, :] = M[768:BG, :768].astype(bf16)
    last = diag(6)
    for j in range(6):
        s_ref[352:368, j * NB:(j + 1) * NB] = last[16 * j:16 * j + 16, :]
    s_ref[368:, :] = jnp.zeros((16, 768), bf16)
    t_ref[...] = s_ref[pl.ds(pl.multiple_of(c * 192, 16), 192), :]


def second_inverse(at, m):
    return pl.pallas_call(
        second_kernel,
        out_shape=jax.ShapeDtypeStruct((192, 768), bf16),
        in_specs=[pl.BlockSpec(memory_space=pltpu.SMEM), pl.BlockSpec(memory_space=pltpu.VMEM)],
        scratch_shapes=[pltpu.VMEM((GP, GP), f32), pltpu.VMEM((NB, NB), f32), pltpu.VMEM((384, 768), bf16)],
        compiler_params=VMEM,
    )(at, m)


def spread(t):
    q = jnp.stack([t] + [in_plane(t, d, True) for d in (1, 2, 3)])
    return jnp.stack([q] + [in_plane(q, d, False) for d in (1, 2, 3)])


def apply_kernel(idx_ref, l_ref, a1, b1, a2, b2, o_ref, s1, s2, lv):
    b = pl.program_id(0)
    c = idx_ref[3 * 16]

    @pl.when(b == 0)
    def _():
        lv[...] = jnp.zeros(lv.shape, bf16)

    s1[pl.ds(pl.multiple_of(c * 128, 128), 128), :] = a1[0]
    s1[pl.ds(pl.multiple_of((1 - c) * 128, 128), 128), :] = b1[0]
    s2[pl.ds(pl.multiple_of(c * 192, 16), 192), :] = a2[0]
    s2[pl.ds(pl.multiple_of((1 - c) * 192, 16), 192), :] = b2[0]
    lv[0:256, 0:256] = s1[:, 0:256]
    lv[256:512, 0:512] = s1[:, 256:768]
    lv[512:864, 0:768] = s2[0:352, :]
    for j in range(6):
        lv[768 + 16 * j:784 + 16 * j, 768:896] = s2[352:368, j * NB:(j + 1) * NB]
    left = l_ref[0]
    y = [
        dot(left[:, :n], lv[r0:r1, :n], 1, 1).astype(bf16)
        for r0, r1, n in ((0, 256, 256), (256, 512, 512), (512, 768, 768), (768, 864, 864))
    ]
    out = []
    for i, (c0, c1) in enumerate(((0, 256), (256, 512), (512, 768), (768, 864))):
        acc = dot(y[i], lv[(0, 256, 512, 768)[i]:(256, 512, 768, 864)[i], c0:c1], 1, 0)
        for k in range(i + 1, 4):
            acc = acc + dot(y[k], lv[(0, 256, 512, 768)[k]:(256, 512, 768, 864)[k], c0:c1], 1, 0)
        out.append(acc.astype(bf16))
    for i in range(4):
        @pl.when(lax.rem(b, 4) == i)
        def _():
            for (c0, c1), v in zip(((0, 256), (256, 512), (512, 768), (768, 864)), out):
                o_ref[:, i * BG + c0:i * BG + c1] = v


def apply(idx, left, one, one_other, two, two_other):
    return pl.pallas_call(
        apply_kernel,
        out_shape=jax.ShapeDtypeStruct((BA, 16 * BG), bf16),
        grid_spec=pltpu.PrefetchScalarGridSpec(
            num_scalar_prefetch=1,
            grid=(16,),
            in_specs=[
                pl.BlockSpec((1, BA, BG), lambda b, s: (s[b], 0, 0)),
                pl.BlockSpec((1, 128, 768), lambda b, s: (s[16 + b], 0, 0)),
                pl.BlockSpec((1, 128, 768), lambda b, s: (s[32 + b], 0, 0)),
                pl.BlockSpec((1, 192, 768), lambda b, s: (s[16 + b], 0, 0)),
                pl.BlockSpec((1, 192, 768), lambda b, s: (s[32 + b], 0, 0)),
            ],
            out_specs=pl.BlockSpec((BA, 4 * BG), lambda b, s: (0, b // 4)),
            scratch_shapes=[
                pltpu.VMEM((256, 768), bf16),
                pltpu.VMEM((384, 768), bf16),
                pltpu.VMEM((BG, GP), bf16),
            ],
        ),
        compiler_params=VMEM,
    )(idx, left, one, one_other, two, two_other)


def shards(layer_inputs, output_grads, weight_grad):
    x, y, zh, zl, c = (lax.axis_index(n) for n in ("x", "y", "zh", "zl", "c"))
    at = jnp.stack([2 * zh + zl, c]).astype(jnp.int32)
    w = weight_grad.reshape(BA, 2, BG).transpose(1, 0, 2)
    w = jnp.concatenate([w, swap_zh(w)], axis=0)
    w = jnp.concatenate([w] + [along_y(w, d) for d in (1, 2, 3)], axis=0)

    t = turn(output_grads, layer_inputs)
    t = lax.all_to_all(t, ("x", "y"), 0, 0, tiled=True)
    mine, other = gram(at, t)
    own, part = sum_over_copies(mine, other)
    m, t1, act = first_inverse(at, own, part)
    act = move(
        act, ("zl", "c", "y"), lambda zl, c, y: (y >> 1, y & 1, 2 * zl + c)
    )
    one = spread(t1).reshape(16, 128, 768)
    one_other = swap_core(one)
    t2 = second_inverse(at, m)
    two = spread(t2).reshape(16, 192, 768)
    two_other = swap_core(two)
    left = lax.dot_general(act, w, (((1,), (1,)), ((), ())), preferred_element_type=f32).astype(bf16)
    left = left.transpose(1, 0, 2)
    b = jnp.arange(16)
    w_at = ((y - (b >> 2)) % 4) * 4 + (zh ^ ((b >> 1) & 1)) * 2 + (b & 1)
    dx, dy = (x - (b >> 2)) % 4, (y - (b & 3)) % 4
    by_x, by_y = dy * 4 + dx, dx * 4 + dy
    idx = jnp.concatenate([
        w_at, jnp.where(c == 0, by_x, by_y), jnp.where(c == 0, by_y, by_x), c[None]
    ]).astype(jnp.int32)
    return apply(idx, left, one, one_other, two, two_other)


def solution(mesh):
    fine = Mesh(np.asarray(mesh.devices).reshape(tuple(SIZES.values())), tuple(SIZES))
    dp, owner = ("x", "zl", "c"), ("y", "zh")
    return jax.shard_map(
        shards,
        mesh=fine,
        in_specs=(P(dp + owner, None), P(dp + owner, None), P(dp, owner)),
        out_specs=P(dp, None),
        check_vma=False,
    )
```

```python
import functools
import jax, jax.numpy as jnp
from jax import lax
from jax.experimental import pallas as pl
from jax.experimental.pallas import tpu as pltpu
f32=jnp.float32; bf16=jnp.bfloat16
NB=128

def split3(x):
    h=x.astype(bf16); r=x-h.astype(f32)
    m=r.astype(bf16); l=(r-m.astype(f32)).astype(bf16)
    return h,m,l

def bc(x,j):
    return jnp.broadcast_to(x[j:j+1,:],(8,128))

def tree(v):
    while len(v)>1:
        v=[a+b for a,b in zip(v[::2],v[1::2])]+([v[-1]] if len(v)%2 else [])
    return v[0]

def eliminate(chains):
    lane=lax.broadcasted_iota(jnp.int32,(8,128),1); sub=lax.broadcasted_iota(jnp.int32,(8,128),0)
    outs=[[] for _ in chains]
    for g in range(16):
        lo=8*g
        ing=(lane>=lo)&(lane<lo+8)
        eye=jnp.where(lane-lo==sub,1.0,0.0).astype(f32)
        st=[]
        for rows in chains:
            R=rows[g]
            B=[jnp.broadcast_to(R[:,lo+j:lo+j+1],(8,128)) for j in range(8)]
            S={(i,q):bc(B[q],i) for q in range(8) for i in range(q+1)}
            st.append([jnp.where(ing,eye,R),B,jnp.zeros((8,128),f32),S])
        for j in range(8):
            for s_ in st:
                R,B,U,S=s_
                p=S[j,j]
                r0=pl.reciprocal(p,approx=True)
                e=2.0-p*r0
                inv=r0*e
                for i in range(j+1,8):
                    for q in range(i,8):
                        S[i,q]=S[i,q]-((S[j,i]*S[j,q])*r0)*e
                rs=lax.rsqrt(p)
                rs=rs*(1.5-0.5*p*rs*rs)
                b=bc(R,j)
                U=jnp.where(sub==j,b*rs,U)
                m=b*inv
                R=jnp.where(sub==j,m,R-B[j]*m)
                for q in range(j+1,8):
                    s=S[j,q]*inv
                    B[q]=jnp.where(sub==j,s,B[q]-B[j]*s)
                s_[0]=R; s_[2]=U
        for ci,(rows,s_) in enumerate(zip(chains,st)):
            W=s_[0]; outs[ci].append(s_[2])
            w=[bc(W,j) for j in range(8)]
            for i in range(g+1,16):
                a=rows[i]
                rows[i]=jnp.where(ing,0.0,a)-tree([jnp.broadcast_to(a[:,lo+j:lo+j+1],(8,128))*w[j] for j in range(8)])
    return outs

def dot(a,b,ca,cb):
    return lax.dot_general(a,b,(((ca,),(cb,)),((),())),preferred_element_type=f32)

def load_diag(M,k,off=0):
    cols=pl.ds(pl.multiple_of(k*NB,NB),NB)
    return [M[pl.ds(pl.multiple_of((k-off)*NB+8*i,8),8),cols] for i in range(16)]

def store_lower(LD,rows):
    lane=lax.broadcasted_iota(jnp.int32,(8,128),1); sub=lax.broadcasted_iota(jnp.int32,(8,128),0)
    for i,u in enumerate(rows):
        LD[8*i:8*i+8,:]=jnp.where(lane<=sub+8*i,u,0.0)

def eye(n):
    return jnp.where(lax.broadcasted_iota(jnp.int32,(n,n),0)==lax.broadcasted_iota(jnp.int32,(n,n),1),1.0,0.0).astype(f32)

def panel(M,LD,k,n,off=0):
    nb=n//NB; c0=k*NB; r0=c0-off*NB
    M[r0:r0+NB,c0:c0+NB]=eye(NB)
    lh,lm,ll=split3(LD[...])
    mh,mm,ml=split3(M[r0:r0+NB,:])
    hm=jnp.concatenate([mh,mm],0); lhh=jnp.concatenate([ml,mh],0)
    U=dot(jnp.concatenate([lh,lh],1),hm,1,0)+dot(jnp.concatenate([lm,lm],1),hm,1,0)+dot(jnp.concatenate([lh,ll],1),lhh,1,0)
    M[r0:r0+NB,:]=U
    if k+1<nb:
        h,m,l=split3(U)
        c,r=c0+NB,r0+NB
        hm=jnp.concatenate([h,m],0); lhh=jnp.concatenate([l,h],0)
        ht,mt,lt=h[:,c:].T,m[:,c:].T,l[:,c:].T
        S=dot(jnp.concatenate([ht,ht],1),hm,1,0)+dot(jnp.concatenate([mt,mt],1),hm,1,0)+dot(jnp.concatenate([ht,lt],1),lhh,1,0)
        M[r:,c0:c]=jnp.zeros((n-c,NB),f32)
        M[r:,:]=M[r:,:]-S

def each(k,ks,f):
    for kk in ks:
        @pl.when(k==kk)
        def _(): f(kk)

def steps(M,LD,n,ks,off=0,Ma=None,LDa=None,na=0):
    def body(k,_):
        blocks=[load_diag(M,k,off)]
        if Ma is not None: blocks.append(load_diag(Ma,k-ks[0]))
        out=eliminate(blocks)
        store_lower(LD,out[0])
        if Ma is not None: store_lower(LDa,out[1])
        def both(kk):
            panel(M,LD,kk,n,off)
            if Ma is not None: panel(Ma,LDa,kk-ks[0],na)
        each(k,ks,both)
        return 0
    lax.fori_loop(ks[0],ks[-1]+1,body,0)


import itertools
import math
import numpy as np
from jax.sharding import Mesh, PartitionSpec as P

BA = 320
BG = 864
GP = 896
AP = 384
TOKENS = 16384.0
DAMPING = 0.1
SIZES = dict(x=4, zl=2, c=2, y=4, zh=2)
GB = [(i, j) for i in range(GP // NB) for j in range(i, GP // NB)]
AB = [(i, j) for i in range(AP // NB) for j in range(i, AP // NB)]
ROWS = len(GB) * NB
CHUNK = ROWS // 8
VMEM = pltpu.CompilerParams(vmem_limit_bytes=56 << 20)


def move(a, names, target):
    dims = [SIZES[n] for n in names]
    pairs = []
    for at in itertools.product(*map(range, dims)):
        to = target(*at)
        pairs.append((int(np.ravel_multi_index(at, dims)), int(np.ravel_multi_index(to, dims))))
    return lax.ppermute(a, names, pairs)


def along_z(a, d):
    def target(zl, zh):
        z = (2 * zh + zl + d) % 4
        return z % 2, z // 2
    return move(a, ("zl", "zh"), target)


def along_y(a, d):
    return move(a, ("y",), lambda y: ((y + d) % 4,))


def swap_core(a):
    return move(a, ("c",), lambda c: (1 - c,))


def swap_zh(a):
    return move(a, ("zh",), lambda h: (1 - h,))


def in_plane(a, d, first):
    def target(x, c, y):
        return ((x + d) % 4, c, y) if (c == 0) == first else (x, c, (y + d) % 4)
    return move(a, ("x", "c", "y"), target)


def cost(us):
    return pl.CostEstimate(flops=int(us * 1e9), bytes_accessed=1 << 20, transcendentals=0)


def turn_kernel(size, slot, g_ref, o_ref):
    for t in range(g_ref.shape[1] // NB):
        tile = g_ref[:, t * NB:(t + 1) * NB].T
        at, end = t * NB, (t + 1) * NB
        while at < end:
            b = at // size
            stop = min(end, (b + 1) * size)
            o_ref[slot(b), at - b * size:stop - b * size, :] = tile[at - t * NB:stop - t * NB, :]
            at = stop


def turn(g, size, slot, us):
    return pl.pallas_call(
        functools.partial(turn_kernel, size, slot),
        out_shape=jax.ShapeDtypeStruct((16, size, NB), bf16),
        compiler_params=VMEM,
        cost_estimate=cost(us),
    )(g)


def products(t_ref, s_ref, p_ref, size, n, blocks):
    if size < n:
        s_ref[size:, :] = jnp.zeros((n - size, 16 * NB), bf16)
    for s in range(16):
        s_ref[:size, s * NB:(s + 1) * NB] = t_ref[s]
    for r0 in range(0, n, 2 * NB):
        rows = min(2 * NB, n - r0)
        d = dot(s_ref[r0:r0 + rows, :], s_ref[r0:, :], 1, 1)
        for k, (i, j) in enumerate(blocks):
            if r0 <= i * NB < r0 + rows:
                p_ref[k * NB:(k + 1) * NB, :] = d[i * NB - r0:(i + 1) * NB - r0, j * NB - r0:(j + 1) * NB - r0]


def gram_kernel(at_ref, t_ref, mine_ref, other_ref, s_ref, p_ref):
    z, c = at_ref[0], at_ref[1]
    products(t_ref, s_ref, p_ref, BG, GP, GB)
    for q in range(4):
        d = lax.rem(q - z + 4, 4)
        rows = pl.ds(pl.multiple_of(d * CHUNK, 8), CHUNK)
        first, second = p_ref[q * CHUNK:(q + 1) * CHUNK, :], p_ref[(4 + q) * CHUNK:(5 + q) * CHUNK, :]
        mine_ref[rows, :] = jnp.where(c == 0, first, second)
        other_ref[rows, :] = jnp.where(c == 0, second, first)


def gram(at, t):
    half = jax.ShapeDtypeStruct((4 * CHUNK, NB), f32)
    return pl.pallas_call(
        gram_kernel,
        out_shape=(half, half),
        in_specs=[pl.BlockSpec(memory_space=pltpu.SMEM), pl.BlockSpec(memory_space=pltpu.VMEM)],
        scratch_shapes=[pltpu.VMEM((GP, 16 * NB), bf16), pltpu.VMEM((ROWS, NB), f32)],
        compiler_params=VMEM,
        cost_estimate=cost(8),
    )(at, t)


def small_gram_kernel(t_ref, p_ref, s_ref):
    products(t_ref, s_ref, p_ref, BA, AP, AB)


def small_gram(t):
    return pl.pallas_call(
        small_gram_kernel,
        out_shape=jax.ShapeDtypeStruct((len(AB) * NB, NB), f32),
        scratch_shapes=[pltpu.VMEM((AP, 16 * NB), bf16)],
        compiler_params=VMEM,
        cost_estimate=cost(3),
    )(t)


def sum_over_copies(mine, other):
    h = mine + swap_core(other)
    part = [h[d * CHUNK:(d + 1) * CHUNK] for d in range(4)]
    got = [along_z(part[d], d) for d in (1, 2, 3)]
    s = part[0] + got[0] + got[1] + got[2]
    own = jnp.concatenate([s] + [along_z(s, d) for d in (1, 2, 3)], axis=0)
    return own, swap_core(own)


def small_sum(p, c):
    half = len(AB) * NB // 2
    first, second = p[:half], p[half:]
    h = jnp.where(c == 0, first, second) + swap_core(jnp.where(c == 0, second, first))
    got = [along_y(h, d) for d in (1, 2, 3)]
    s = (h + got[1]) + (got[0] + got[2])
    o = swap_core(s)
    return jnp.concatenate([jnp.where(c == 0, s, o), jnp.where(c == 0, o, s)], axis=0)


def unpack(M, n, blocks, p_ref):
    M[...] = jnp.zeros((n, n), f32)
    for k, (i, j) in enumerate(blocks):
        block = p_ref[k * NB:(k + 1) * NB, :] / TOKENS
        if i == j:
            block = block + DAMPING * eye(NB)
        M[i * NB:(i + 1) * NB, j * NB:(j + 1) * NB] = block


def lower():
    return lax.broadcasted_iota(jnp.int32, (NB, NB), 0) >= lax.broadcasted_iota(jnp.int32, (NB, NB), 1)


TOP = 512
REST = BG - TOP
PACK = 128 + 256 + REST


def tidy(M, n):
    for i in range(n // NB):
        M[i * NB:(i + 1) * NB, i * NB:(i + 1) * NB] = jnp.where(lower(), M[i * NB:(i + 1) * NB, i * NB:(i + 1) * NB], 0.0)


def first_kernel(at_ref, own_ref, part_ref, m_ref, t_ref, p_ref, M, LD, s_ref):
    z, c = at_ref[0], at_ref[1]
    for d in range(4):
        q = lax.rem(z - d + 4, 4)
        p_ref[pl.ds(pl.multiple_of((4 * c + q) * CHUNK, 8), CHUNK), :] = own_ref[d * CHUNK:(d + 1) * CHUNK, :]
        p_ref[pl.ds(pl.multiple_of((4 * (1 - c) + q) * CHUNK, 8), CHUNK), :] = part_ref[d * CHUNK:(d + 1) * CHUNK, :]
    unpack(M, GP, GB, p_ref)
    steps(M, LD, GP, range(4))
    m_ref[...] = M[TOP:, TOP:]
    tidy(M, TOP)
    for i in (0, 2):
        M[i * NB:(i + 1) * NB, (i + 1) * NB:(i + 2) * NB] = jnp.zeros((NB, NB), f32)
    s_ref[0:128, 0:256] = M[0:128, 0:256].astype(bf16)
    s_ref[0:128, 256:512] = M[128:256, 0:256].astype(bf16)
    s_ref[128:384, :] = M[256:512, :TOP].astype(bf16)
    s_ref[384:, :] = M[TOP:BG, :TOP].astype(bf16)
    t_ref[...] = s_ref[pl.ds(pl.multiple_of(c * (PACK // 2), 16), PACK // 2), :]


def first_inverse(at, own, part):
    return pl.pallas_call(
        first_kernel,
        out_shape=(jax.ShapeDtypeStruct((AP, AP), f32), jax.ShapeDtypeStruct((PACK // 2, TOP), bf16)),
        in_specs=[pl.BlockSpec(memory_space=pltpu.SMEM)] + [pl.BlockSpec(memory_space=pltpu.VMEM)] * 2,
        scratch_shapes=[
            pltpu.VMEM((ROWS, NB), f32),
            pltpu.VMEM((GP, GP), f32),
            pltpu.VMEM((NB, NB), f32),
            pltpu.VMEM((PACK, TOP), bf16),
        ],
        compiler_params=VMEM,
        cost_estimate=cost(2),
    )(at, own, part)


def second_kernel(m_in, t_ref, M, LD):
    M[...] = m_in[...]
    steps(M, LD, AP, range(3))
    tidy(M, AP)
    at = 0
    for i in range(3):
        rows = min(NB, REST - i * NB)
        for j in range(i + 1):
            t_ref[at:at + rows, :] = M[i * NB:i * NB + rows, j * NB:(j + 1) * NB].astype(bf16)
            at += rows


LAST = 3 * NB + 3 * (REST - 2 * NB)


def second_inverse(m):
    return pl.pallas_call(
        second_kernel,
        out_shape=jax.ShapeDtypeStruct((LAST, NB), bf16),
        scratch_shapes=[pltpu.VMEM((AP, AP), f32), pltpu.VMEM((NB, NB), f32)],
        compiler_params=VMEM,
        cost_estimate=cost(20),
    )(m)


def small_inverse_kernel(a_in, inv_ref, M, LD):
    unpack(M, AP, AB, a_in)
    steps(M, LD, AP, range(3))
    tidy(M, AP)
    n = AP // NB
    for i in range(n):
        for j in range(i + 1, n):
            M[i * NB:(i + 1) * NB, j * NB:(j + 1) * NB] = jnp.zeros((NB, NB), f32)
    L = M[:BA, :BA]
    inv_ref[...] = lax.dot_general(
        L, L, (((0,), (0,)), ((), ())), precision=lax.Precision.HIGHEST, preferred_element_type=f32
    ).astype(bf16)


def small_inverse(a):
    return pl.pallas_call(
        small_inverse_kernel,
        out_shape=jax.ShapeDtypeStruct((BA, BA), bf16),
        scratch_shapes=[pltpu.VMEM((AP, AP), f32), pltpu.VMEM((NB, NB), f32)],
        compiler_params=VMEM,
        cost_estimate=cost(1),
    )(a)


def near(t):
    return jnp.stack([t] + [in_plane(t, d, True) for d in (1, 2, 3)])


def far(q):
    return [q] + [in_plane(q, d, False) for d in (1, 2, 3)]


def left_kernel(at_ref, act_ref, *refs):
    w, (o_ref, wv, sem) = refs[0:5], refs[5:]
    d, zh = pl.program_id(0), at_ref[2]

    def copies(k):
        if k == 2:
            return [
                pltpu.make_async_copy(w[2], wv.at[2, 0:2], sem.at[2]),
                pltpu.make_async_copy(w[3], wv.at[2, 2:4], sem.at[4]),
            ]
        return [pltpu.make_async_copy(w[(0, 1, None, 4)[k]], wv.at[k], sem.at[k])]

    @pl.when(d == 0)
    def _():
        for k in range(4):
            for m in copies(k):
                m.start()

    for k in range(4):
        @pl.when(d == k)
        def _():
            for m in copies(k):
                m.wait()
    for xb in range(4):
        zb, h = xb // 2, xb % 2
        o_ref[0, xb] = dot(act_ref[...], wv[d, 2 * jnp.where(zh == zb, 0, 1) + h], 1, 0).astype(bf16)


def left_rows(at, act, w):
    return pl.pallas_call(
        left_kernel,
        out_shape=jax.ShapeDtypeStruct((4, 4, BA, BG), bf16),
        grid_spec=pltpu.PrefetchScalarGridSpec(
            num_scalar_prefetch=1,
            grid=(4,),
            in_specs=[pl.BlockSpec((BA, BA), lambda d, s: (0, 0))] + [pl.BlockSpec(memory_space=pl.ANY)] * 5,
            out_specs=pl.BlockSpec((1, 4, BA, BG), lambda d, s: (d, 0, 0, 0)),
            scratch_shapes=[pltpu.VMEM((4, 4, BA, BG), bf16), pltpu.SemaphoreType.DMA((5,))],
        ),
        compiler_params=VMEM,
        cost_estimate=cost(8),
    )(at, act, *w)


def apply_kernel(at_ref, l_ref, *refs):
    own, part, two = refs[0:4], refs[4:8], refs[8:12]
    o_ref, va, vb, v, t0, t1, K, sema, semb = refs[12:]
    x, c = at_ref[0], at_ref[3]
    d = pl.program_id(0)
    slot = lax.rem(d, 2)

    def fetch(k):
        for core in range(2):
            @pl.when(c == core)
            def _():
                first, second = (own, part) if core == 0 else (part, own)
                pltpu.make_async_copy(first[k], va.at[k % 2], sema.at[k % 2]).start()
                for q in range(4):
                    pltpu.make_async_copy(second[q].at[k], vb.at[k % 2, q], semb.at[k % 2, q]).start()

    @pl.when(d == 0)
    def _():
        fetch(0)
        K[...] = jnp.zeros(K.shape, bf16)
        for k in range(4):
            v[k] = two[k][...]

    for k in range(3):
        @pl.when(d == k)
        def _():
            fetch(k + 1)

    pltpu.make_async_copy(own[0], va.at[slot], sema.at[slot]).wait()
    for q in range(4):
        pltpu.make_async_copy(own[0].at[0], vb.at[slot, q], semb.at[slot, q]).wait()

    half = PACK // 2
    for xb in range(4):
        dx = lax.rem(x - xb + 4, 4)
        s = xb % 2
        t0[s, 0:128, :] = va[slot, dx, 0:128, 0:256]
        t0[s, 128:256, :] = va[slot, dx, 0:128, 256:512]
        t1[s, 0:half - 128, :] = va[slot, dx, 128:half, :]
        t1[s, half - 128:256, :] = vb[slot, dx, 0:384 - half, :]
        k = v.at[jnp.where(c == 0, d, dx), jnp.where(c == 0, dx, d)]
        at = 0
        for i in range(3):
            rows = min(NB, REST - i * NB)
            for j in range(i + 1):
                K[s, i * NB:i * NB + rows, j * NB:(j + 1) * NB] = k[at:at + rows, :]
                at += rows
        e = vb[slot, dx, 384 - half:half, :]
        kk = K[s][:, :REST]
        left = l_ref[0, xb]
        l0 = left[:, :TOP]
        u = (left[:, TOP:].astype(f32) + dot(l0, e, 1, 1)).astype(bf16)
        y0 = dot(l0[:, :256], t0[s], 1, 1).astype(bf16)
        y1 = dot(l0, t1[s], 1, 1).astype(bf16)
        g = dot(dot(u, kk, 1, 1).astype(bf16), kk, 1, 0).astype(bf16)
        r = dot(y1, t1[s], 1, 0) + dot(g, e, 1, 0)
        o_ref[:, xb * BG:xb * BG + 256] = (r[:, :256] + dot(y0, t0[s], 1, 0)).astype(bf16)
        o_ref[:, xb * BG + 256:xb * BG + TOP] = r[:, 256:].astype(bf16)
        o_ref[:, xb * BG + TOP:(xb + 1) * BG] = g


def apply(at, left, own, part, two):
    any_space = pl.BlockSpec(memory_space=pl.ANY)
    return pl.pallas_call(
        apply_kernel,
        out_shape=jax.ShapeDtypeStruct((BA, 16 * BG), bf16),
        grid_spec=pltpu.PrefetchScalarGridSpec(
            num_scalar_prefetch=1,
            grid=(4,),
            in_specs=[pl.BlockSpec((1, 4, BA, BG), lambda d, s: (d, 0, 0, 0))]
            + [any_space] * 8
            + [pl.BlockSpec((4, LAST, NB), lambda d, s: (0, 0, 0))] * 4,
            out_specs=pl.BlockSpec((BA, 4 * BG), lambda d, s: (0, lax.rem(s[1] - d + 4, 4))),
            scratch_shapes=[
                pltpu.VMEM((2, 4, PACK // 2, TOP), bf16),
                pltpu.VMEM((2, 4, PACK // 2, TOP), bf16),
                pltpu.VMEM((4, 4, LAST, NB), bf16),
                pltpu.VMEM((2, 256, 256), bf16),
                pltpu.VMEM((2, 256, TOP), bf16),
                pltpu.VMEM((2, REST, AP), bf16),
                pltpu.SemaphoreType.DMA((2,)),
                pltpu.SemaphoreType.DMA((2, 4)),
            ],
        ),
        compiler_params=VMEM,
        cost_estimate=cost(25),
    )(at, left, *own, *part, *two)


def tie(*arrays):
    return lax.optimization_barrier(arrays)


def shards(layer_inputs, output_grads, weight_grad):
    x, y, zh, zl, c = (lax.axis_index(n) for n in ("x", "y", "zh", "zl", "c"))
    zc = jnp.stack([2 * zh + zl, c]).astype(jnp.int32)
    at = jnp.stack([x, y, zh, c]).astype(jnp.int32)

    t = turn(output_grads, BG, lambda b: 4 * (b % 4) + b // 4, 5)
    t, weight_grad, layer_inputs = tie(t, weight_grad, layer_inputs)
    t = lax.all_to_all(t, ("x", "y"), 0, 0, tiled=True)
    w = weight_grad.reshape(BA, 2, BG).transpose(1, 0, 2)
    w_far = swap_zh(w)
    u = turn(layer_inputs, BA, lambda b: b, 2)
    w = jnp.concatenate([w, w_far], axis=0)
    t, w, u = tie(t, w, u)
    w1, w3 = along_y(w, 1), along_y(w, 3)
    mine, other = gram(zc, t)
    mine, other, u = tie(mine, other, u)
    u = lax.all_to_all(u, ("x", "zl", "zh"), 0, 0, tiled=True)
    own, part = sum_over_copies(mine, other)
    m, t1 = first_inverse(zc, own, part)
    m, t1, w1, w3, u = tie(m, t1, w1, w3, u)
    w2 = [along_y(w1[:2], 1), along_y(w3[2:], 3)]
    q1 = near(t1)
    a = small_gram(u)
    m, q1, a = tie(m, q1, a)
    one = far(q1)
    q1_other = swap_core(q1)
    a = small_sum(a, c)
    t2 = second_inverse(m)
    t2, a, q1_other = tie(t2, a, q1_other)
    act = small_inverse(a)
    t2, act, *rest = tie(t2, act, *w2, *one)
    w2, one = rest[:2], rest[2:]
    two = far(near(t2))
    act = move(act, ("c", "zh"), lambda c, zh: (zh, c))
    left = left_rows(at, act, [w, w1, *w2, w3])
    one_other = [q1_other] + [swap_core(v) for v in one[1:]]
    return apply(at, left, one, one_other, two)


def solution(mesh):
    fine = Mesh(np.asarray(mesh.devices).reshape(tuple(SIZES.values())), tuple(SIZES))
    dp, owner = ("x", "zl", "c"), ("y", "zh")
    return jax.shard_map(
        shards,
        mesh=fine,
        in_specs=(P(dp + owner, None), P(dp + owner, None), P(dp, owner)),
        out_specs=P(dp, None),
        check_vma=False,
    )
```

```python
import functools
import jax, jax.numpy as jnp
from jax import lax
from jax.experimental import pallas as pl
from jax.experimental.pallas import tpu as pltpu
f32=jnp.float32; bf16=jnp.bfloat16
NB=128

def split3(x):
    h=x.astype(bf16); r=x-h.astype(f32)
    m=r.astype(bf16); l=(r-m.astype(f32)).astype(bf16)
    return h,m,l

def bc(x,j):
    return jnp.broadcast_to(x[j:j+1,:],(8,128))

def tree(v):
    while len(v)>1:
        v=[a+b for a,b in zip(v[::2],v[1::2])]+([v[-1]] if len(v)%2 else [])
    return v[0]

def eliminate(chains):
    lane=lax.broadcasted_iota(jnp.int32,(8,128),1); sub=lax.broadcasted_iota(jnp.int32,(8,128),0)
    outs=[[] for _ in chains]
    for g in range(16):
        lo=8*g
        ing=(lane>=lo)&(lane<lo+8)
        eye=jnp.where(lane-lo==sub,1.0,0.0).astype(f32)
        st=[]
        for rows in chains:
            R=rows[g]
            B=[jnp.broadcast_to(R[:,lo+j:lo+j+1],(8,128)) for j in range(8)]
            S={(i,q):bc(B[q],i) for q in range(8) for i in range(q+1)}
            st.append([jnp.where(ing,eye,R),B,jnp.zeros((8,128),f32),S])
        for j in range(8):
            for s_ in st:
                R,B,U,S=s_
                p=S[j,j]
                r0=pl.reciprocal(p,approx=True)
                e=2.0-p*r0
                inv=r0*e
                for i in range(j+1,8):
                    for q in range(i,8):
                        S[i,q]=S[i,q]-((S[j,i]*S[j,q])*r0)*e
                rs=lax.rsqrt(p)
                rs=rs*(1.5-0.5*p*rs*rs)
                b=bc(R,j)
                U=jnp.where(sub==j,b*rs,U)
                m=b*inv
                R=jnp.where(sub==j,m,R-B[j]*m)
                for q in range(j+1,8):
                    s=S[j,q]*inv
                    B[q]=jnp.where(sub==j,s,B[q]-B[j]*s)
                s_[0]=R; s_[2]=U
        for ci,(rows,s_) in enumerate(zip(chains,st)):
            W=s_[0]; outs[ci].append(s_[2])
            w=[bc(W,j) for j in range(8)]
            for i in range(g+1,16):
                a=rows[i]
                rows[i]=jnp.where(ing,0.0,a)-tree([jnp.broadcast_to(a[:,lo+j:lo+j+1],(8,128))*w[j] for j in range(8)])
    return outs

def dot(a,b,ca,cb):
    return lax.dot_general(a,b,(((ca,),(cb,)),((),())),preferred_element_type=f32)

def load_diag(M,k,off=0):
    cols=pl.ds(pl.multiple_of(k*NB,NB),NB)
    return [M[pl.ds(pl.multiple_of((k-off)*NB+8*i,8),8),cols] for i in range(16)]

def store_lower(LD,rows):
    lane=lax.broadcasted_iota(jnp.int32,(8,128),1); sub=lax.broadcasted_iota(jnp.int32,(8,128),0)
    for i,u in enumerate(rows):
        LD[8*i:8*i+8,:]=jnp.where(lane<=sub+8*i,u,0.0)

def eye(n):
    return jnp.where(lax.broadcasted_iota(jnp.int32,(n,n),0)==lax.broadcasted_iota(jnp.int32,(n,n),1),1.0,0.0).astype(f32)

def panel(M,LD,k,n,off=0):
    nb=n//NB; c0=k*NB; r0=c0-off*NB
    M[r0:r0+NB,c0:c0+NB]=eye(NB)
    lh,lm,ll=split3(LD[...])
    mh,mm,ml=split3(M[r0:r0+NB,:])
    hm=jnp.concatenate([mh,mm],0); lhh=jnp.concatenate([ml,mh],0)
    U=dot(jnp.concatenate([lh,lh],1),hm,1,0)+dot(jnp.concatenate([lm,lm],1),hm,1,0)+dot(jnp.concatenate([lh,ll],1),lhh,1,0)
    M[r0:r0+NB,:]=U
    if k+1<nb:
        h,m,l=split3(U)
        c,r=c0+NB,r0+NB
        hm=jnp.concatenate([h,m],0); lhh=jnp.concatenate([l,h],0)
        ht,mt,lt=h[:,c:].T,m[:,c:].T,l[:,c:].T
        S=dot(jnp.concatenate([ht,ht],1),hm,1,0)+dot(jnp.concatenate([mt,mt],1),hm,1,0)+dot(jnp.concatenate([ht,lt],1),lhh,1,0)
        M[r:,c0:c]=jnp.zeros((n-c,NB),f32)
        M[r:,:]=M[r:,:]-S

def each(k,ks,f):
    for kk in ks:
        @pl.when(k==kk)
        def _(): f(kk)

def steps(M,LD,n,ks,off=0,Ma=None,LDa=None,na=0):
    def body(k,_):
        blocks=[load_diag(M,k,off)]
        if Ma is not None: blocks.append(load_diag(Ma,k-ks[0]))
        out=eliminate(blocks)
        store_lower(LD,out[0])
        if Ma is not None: store_lower(LDa,out[1])
        def both(kk):
            panel(M,LD,kk,n,off)
            if Ma is not None: panel(Ma,LDa,kk-ks[0],na)
        each(k,ks,both)
        return 0
    lax.fori_loop(ks[0],ks[-1]+1,body,0)


import itertools
import math
import numpy as np
from jax.sharding import Mesh, PartitionSpec as P

BA = 320
BG = 864
GP = 896
AP = 384
TOKENS = 16384.0
DAMPING = 0.1
SIZES = dict(x=4, zl=2, c=2, y=4, zh=2)
GB = [(i, j) for i in range(GP // NB) for j in range(i, GP // NB)]
AB = [(i, j) for i in range(AP // NB) for j in range(i, AP // NB)]
ROWS = len(GB) * NB
CHUNK = ROWS // 8
VMEM = pltpu.CompilerParams(vmem_limit_bytes=56 << 20)


def move(a, names, target):
    dims = [SIZES[n] for n in names]
    pairs = []
    for at in itertools.product(*map(range, dims)):
        to = target(*at)
        pairs.append((int(np.ravel_multi_index(at, dims)), int(np.ravel_multi_index(to, dims))))
    return lax.ppermute(a, names, pairs)


def along_z(a, d):
    def target(zl, zh):
        z = (2 * zh + zl + d) % 4
        return z % 2, z // 2
    return move(a, ("zl", "zh"), target)


def along_y(a, d):
    return move(a, ("y",), lambda y: ((y + d) % 4,))


def swap_core(a):
    return move(a, ("c",), lambda c: (1 - c,))


def swap_zh(a):
    return move(a, ("zh",), lambda h: (1 - h,))


def in_plane(a, d, first):
    def target(x, c, y):
        return ((x + d) % 4, c, y) if (c == 0) == first else (x, c, (y + d) % 4)
    return move(a, ("x", "c", "y"), target)


def cost(us):
    return pl.CostEstimate(flops=int(us * 1e9), bytes_accessed=1 << 20, transcendentals=0)


def turn_kernel(size, slot, g_ref, o_ref):
    for t in range(g_ref.shape[1] // NB):
        tile = g_ref[:, t * NB:(t + 1) * NB].T
        at, end = t * NB, (t + 1) * NB
        while at < end:
            b = at // size
            stop = min(end, (b + 1) * size)
            o_ref[slot(b), at - b * size:stop - b * size, :] = tile[at - t * NB:stop - t * NB, :]
            at = stop


def turn(g, size, slot, us):
    return pl.pallas_call(
        functools.partial(turn_kernel, size, slot),
        out_shape=jax.ShapeDtypeStruct((16, size, NB), bf16),
        compiler_params=VMEM,
        cost_estimate=cost(us),
    )(g)


def products(t_ref, s_ref, p_ref, size, n, blocks):
    if size < n:
        s_ref[size:, :] = jnp.zeros((n - size, 16 * NB), bf16)
    for s in range(16):
        s_ref[:size, s * NB:(s + 1) * NB] = t_ref[s]
    for r0 in range(0, n, 2 * NB):
        rows = min(2 * NB, n - r0)
        d = dot(s_ref[r0:r0 + rows, :], s_ref[r0:, :], 1, 1)
        for k, (i, j) in enumerate(blocks):
            if r0 <= i * NB < r0 + rows:
                p_ref[k * NB:(k + 1) * NB, :] = d[i * NB - r0:(i + 1) * NB - r0, j * NB - r0:(j + 1) * NB - r0]


def gram_kernel(at_ref, t_ref, mine_ref, other_ref, s_ref, p_ref):
    z, c = at_ref[0], at_ref[1]
    products(t_ref, s_ref, p_ref, BG, GP, GB)
    for q in range(4):
        d = lax.rem(q - z + 4, 4)
        rows = pl.ds(pl.multiple_of(d * CHUNK, 8), CHUNK)
        first, second = p_ref[q * CHUNK:(q + 1) * CHUNK, :], p_ref[(4 + q) * CHUNK:(5 + q) * CHUNK, :]
        mine_ref[rows, :] = jnp.where(c == 0, first, second)
        other_ref[rows, :] = jnp.where(c == 0, second, first)


def gram(at, t):
    half = jax.ShapeDtypeStruct((4 * CHUNK, NB), f32)
    return pl.pallas_call(
        gram_kernel,
        out_shape=(half, half),
        in_specs=[pl.BlockSpec(memory_space=pltpu.SMEM), pl.BlockSpec(memory_space=pltpu.VMEM)],
        scratch_shapes=[pltpu.VMEM((GP, 16 * NB), bf16), pltpu.VMEM((ROWS, NB), f32)],
        compiler_params=VMEM,
        cost_estimate=cost(8),
    )(at, t)


def small_gram_kernel(t_ref, p_ref, s_ref):
    products(t_ref, s_ref, p_ref, BA, AP, AB)


def small_gram(t):
    return pl.pallas_call(
        small_gram_kernel,
        out_shape=jax.ShapeDtypeStruct((len(AB) * NB, NB), f32),
        scratch_shapes=[pltpu.VMEM((AP, 16 * NB), bf16)],
        compiler_params=VMEM,
        cost_estimate=cost(3),
    )(t)


def sum_over_copies(mine, other):
    h = mine + swap_core(other)
    part = [h[d * CHUNK:(d + 1) * CHUNK] for d in range(4)]
    got = [along_z(part[d], d) for d in (1, 2, 3)]
    s = part[0] + got[0] + got[1] + got[2]
    own = jnp.concatenate([s] + [along_z(s, d) for d in (1, 2, 3)], axis=0)
    return own, swap_core(own)


def small_sum(p, c):
    half = len(AB) * NB // 2
    first, second = p[:half], p[half:]
    h = jnp.where(c == 0, first, second) + swap_core(jnp.where(c == 0, second, first))
    got = [along_z(h, d) for d in (1, 2, 3)]
    s = (h + got[1]) + (got[0] + got[2])
    o = swap_core(s)
    return jnp.concatenate([jnp.where(c == 0, s, o), jnp.where(c == 0, o, s)], axis=0)


def unpack(M, n, blocks, p_ref):
    M[...] = jnp.zeros((n, n), f32)
    for k, (i, j) in enumerate(blocks):
        block = p_ref[k * NB:(k + 1) * NB, :] / TOKENS
        if i == j:
            block = block + DAMPING * eye(NB)
        M[i * NB:(i + 1) * NB, j * NB:(j + 1) * NB] = block


def lower():
    return lax.broadcasted_iota(jnp.int32, (NB, NB), 0) >= lax.broadcasted_iota(jnp.int32, (NB, NB), 1)


TOP = 512
REST = BG - TOP
PACK = 128 + 256 + REST


def tidy(M, n):
    for i in range(n // NB):
        M[i * NB:(i + 1) * NB, i * NB:(i + 1) * NB] = jnp.where(lower(), M[i * NB:(i + 1) * NB, i * NB:(i + 1) * NB], 0.0)


def first_kernel(at_ref, own_ref, part_ref, m_ref, t_ref, p_ref, M, LD, s_ref):
    z, c = at_ref[0], at_ref[1]
    for d in range(4):
        q = lax.rem(z - d + 4, 4)
        p_ref[pl.ds(pl.multiple_of((4 * c + q) * CHUNK, 8), CHUNK), :] = own_ref[d * CHUNK:(d + 1) * CHUNK, :]
        p_ref[pl.ds(pl.multiple_of((4 * (1 - c) + q) * CHUNK, 8), CHUNK), :] = part_ref[d * CHUNK:(d + 1) * CHUNK, :]
    unpack(M, GP, GB, p_ref)
    steps(M, LD, GP, range(4))
    m_ref[...] = M[TOP:, TOP:]
    tidy(M, TOP)
    for i in (0, 2):
        M[i * NB:(i + 1) * NB, (i + 1) * NB:(i + 2) * NB] = jnp.zeros((NB, NB), f32)
    s_ref[0:128, 0:256] = M[0:128, 0:256].astype(bf16)
    s_ref[0:128, 256:512] = M[128:256, 0:256].astype(bf16)
    s_ref[128:384, :] = M[256:512, :TOP].astype(bf16)
    s_ref[384:, :] = M[TOP:BG, :TOP].astype(bf16)
    t_ref[...] = s_ref[pl.ds(pl.multiple_of(c * (PACK // 2), 16), PACK // 2), :]


def first_inverse(at, own, part):
    return pl.pallas_call(
        first_kernel,
        out_shape=(jax.ShapeDtypeStruct((AP, AP), f32), jax.ShapeDtypeStruct((PACK // 2, TOP), bf16)),
        in_specs=[pl.BlockSpec(memory_space=pltpu.SMEM)] + [pl.BlockSpec(memory_space=pltpu.VMEM)] * 2,
        scratch_shapes=[
            pltpu.VMEM((ROWS, NB), f32),
            pltpu.VMEM((GP, GP), f32),
            pltpu.VMEM((NB, NB), f32),
            pltpu.VMEM((PACK, TOP), bf16),
        ],
        compiler_params=VMEM,
        cost_estimate=cost(2),
    )(at, own, part)


def second_kernel(m_in, t_ref, M, LD):
    M[...] = m_in[...]
    steps(M, LD, AP, range(3))
    tidy(M, AP)
    at = 0
    for i in range(3):
        rows = min(NB, REST - i * NB)
        for j in range(i + 1):
            t_ref[at:at + rows, :] = M[i * NB:i * NB + rows, j * NB:(j + 1) * NB].astype(bf16)
            at += rows


LAST = 3 * NB + 3 * (REST - 2 * NB)


def second_inverse(m):
    return pl.pallas_call(
        second_kernel,
        out_shape=jax.ShapeDtypeStruct((LAST, NB), bf16),
        scratch_shapes=[pltpu.VMEM((AP, AP), f32), pltpu.VMEM((NB, NB), f32)],
        compiler_params=VMEM,
        cost_estimate=cost(1),
    )(m)


def small_inverse_kernel(a_in, inv_ref, M, LD):
    unpack(M, AP, AB, a_in)
    steps(M, LD, AP, range(3))
    tidy(M, AP)
    n = AP // NB
    for i in range(n):
        for j in range(i + 1, n):
            M[i * NB:(i + 1) * NB, j * NB:(j + 1) * NB] = jnp.zeros((NB, NB), f32)
    L = M[:BA, :BA]
    inv_ref[...] = lax.dot_general(
        L, L, (((0,), (0,)), ((), ())), precision=lax.Precision.HIGHEST, preferred_element_type=f32
    ).astype(bf16)


def small_inverse(a):
    return pl.pallas_call(
        small_inverse_kernel,
        out_shape=jax.ShapeDtypeStruct((BA, BA), bf16),
        scratch_shapes=[pltpu.VMEM((AP, AP), f32), pltpu.VMEM((NB, NB), f32)],
        compiler_params=VMEM,
        cost_estimate=cost(1),
    )(a)


def near(t):
    return jnp.stack([t] + [in_plane(t, d, True) for d in (1, 2, 3)])


def far(q):
    return [q] + [in_plane(q, d, False) for d in (1, 2, 3)]


def left_kernel(at_ref, act_ref, *refs):
    w, (o_ref, wv, sem) = refs[0:5], refs[5:]
    d, zh = pl.program_id(0), at_ref[2]

    def copies(k):
        if k == 2:
            return [
                pltpu.make_async_copy(w[2], wv.at[2, 0:2], sem.at[2]),
                pltpu.make_async_copy(w[3], wv.at[2, 2:4], sem.at[4]),
            ]
        return [pltpu.make_async_copy(w[(0, 1, None, 4)[k]], wv.at[k], sem.at[k])]

    @pl.when(d == 0)
    def _():
        for k in range(4):
            for m in copies(k):
                m.start()

    for k in range(4):
        @pl.when(d == k)
        def _():
            for m in copies(k):
                m.wait()
    for xb in range(4):
        zb, h = xb // 2, xb % 2
        o_ref[0, xb] = dot(act_ref[...], wv[d, 2 * jnp.where(zh == zb, 0, 1) + h], 1, 0).astype(bf16)


def left_rows(at, act, w):
    return pl.pallas_call(
        left_kernel,
        out_shape=jax.ShapeDtypeStruct((4, 4, BA, BG), bf16),
        grid_spec=pltpu.PrefetchScalarGridSpec(
            num_scalar_prefetch=1,
            grid=(4,),
            in_specs=[pl.BlockSpec((BA, BA), lambda d, s: (0, 0))] + [pl.BlockSpec(memory_space=pl.ANY)] * 5,
            out_specs=pl.BlockSpec((1, 4, BA, BG), lambda d, s: (d, 0, 0, 0)),
            scratch_shapes=[pltpu.VMEM((4, 4, BA, BG), bf16), pltpu.SemaphoreType.DMA((5,))],
        ),
        compiler_params=VMEM,
        cost_estimate=cost(8),
    )(at, act, *w)


def apply_kernel(at_ref, l_ref, *refs):
    own, part, two = refs[0:4], refs[4:8], refs[8:12]
    o_ref, va, vb, v, t0, t1, K, sema, semb = refs[12:]
    x, c = at_ref[0], at_ref[3]
    d = pl.program_id(0)
    slot = lax.rem(d, 2)

    def fetch(k):
        for core in range(2):
            @pl.when(c == core)
            def _():
                first, second = (own, part) if core == 0 else (part, own)
                pltpu.make_async_copy(first[k], va.at[k % 2], sema.at[k % 2]).start()
                for q in range(4):
                    pltpu.make_async_copy(second[q].at[k], vb.at[k % 2, q], semb.at[k % 2, q]).start()

    @pl.when(d == 0)
    def _():
        fetch(0)
        K[...] = jnp.zeros(K.shape, bf16)
        for k in range(4):
            v[k] = two[k][...]

    for k in range(3):
        @pl.when(d == k)
        def _():
            fetch(k + 1)

    pltpu.make_async_copy(own[0], va.at[slot], sema.at[slot]).wait()
    for q in range(4):
        pltpu.make_async_copy(own[0].at[0], vb.at[slot, q], semb.at[slot, q]).wait()

    half = PACK // 2
    for xb in range(4):
        dx = lax.rem(x - xb + 4, 4)
        s = xb % 2
        t0[s, 0:128, :] = va[slot, dx, 0:128, 0:256]
        t0[s, 128:256, :] = va[slot, dx, 0:128, 256:512]
        t1[s, 0:half - 128, :] = va[slot, dx, 128:half, :]
        t1[s, half - 128:256, :] = vb[slot, dx, 0:384 - half, :]
        k = v.at[jnp.where(c == 0, d, dx), jnp.where(c == 0, dx, d)]
        at = 0
        for i in range(3):
            rows = min(NB, REST - i * NB)
            for j in range(i + 1):
                K[s, i * NB:i * NB + rows, j * NB:(j + 1) * NB] = k[at:at + rows, :]
                at += rows
        e = vb[slot, dx, 384 - half:half, :]
        kk = K[s][:, :REST]
        left = l_ref[0, xb]
        l0 = left[:, :TOP]
        u = (left[:, TOP:].astype(f32) + dot(l0, e, 1, 1)).astype(bf16)
        y0 = dot(l0[:, :256], t0[s], 1, 1).astype(bf16)
        y1 = dot(l0, t1[s], 1, 1).astype(bf16)
        g = dot(dot(u, kk, 1, 1).astype(bf16), kk, 1, 0).astype(bf16)
        r = dot(y1, t1[s], 1, 0) + dot(g, e, 1, 0)
        o_ref[:, xb * BG:xb * BG + 256] = (r[:, :256] + dot(y0, t0[s], 1, 0)).astype(bf16)
        o_ref[:, xb * BG + 256:xb * BG + TOP] = r[:, 256:].astype(bf16)
        o_ref[:, xb * BG + TOP:(xb + 1) * BG] = g


def apply(at, left, own, part, two):
    any_space = pl.BlockSpec(memory_space=pl.ANY)
    return pl.pallas_call(
        apply_kernel,
        out_shape=jax.ShapeDtypeStruct((BA, 16 * BG), bf16),
        grid_spec=pltpu.PrefetchScalarGridSpec(
            num_scalar_prefetch=1,
            grid=(4,),
            in_specs=[pl.BlockSpec((1, 4, BA, BG), lambda d, s: (d, 0, 0, 0))]
            + [any_space] * 8
            + [pl.BlockSpec((4, LAST, NB), lambda d, s: (0, 0, 0))] * 4,
            out_specs=pl.BlockSpec((BA, 4 * BG), lambda d, s: (0, lax.rem(s[1] - d + 4, 4))),
            scratch_shapes=[
                pltpu.VMEM((2, 4, PACK // 2, TOP), bf16),
                pltpu.VMEM((2, 4, PACK // 2, TOP), bf16),
                pltpu.VMEM((4, 4, LAST, NB), bf16),
                pltpu.VMEM((2, 256, 256), bf16),
                pltpu.VMEM((2, 256, TOP), bf16),
                pltpu.VMEM((2, REST, AP), bf16),
                pltpu.SemaphoreType.DMA((2,)),
                pltpu.SemaphoreType.DMA((2, 4)),
            ],
        ),
        compiler_params=VMEM,
        cost_estimate=cost(25),
    )(at, left, *own, *part, *two)


def tie(*arrays):
    return lax.optimization_barrier(arrays)


def shards(layer_inputs, output_grads, weight_grad):
    x, y, zh, zl, c = (lax.axis_index(n) for n in ("x", "y", "zh", "zl", "c"))
    zc = jnp.stack([2 * zh + zl, c]).astype(jnp.int32)
    at = jnp.stack([x, y, zh, c]).astype(jnp.int32)

    t = turn(output_grads, BG, lambda b: 4 * (b % 4) + b // 4, 5)
    t, weight_grad, layer_inputs = tie(t, weight_grad, layer_inputs)
    t = lax.all_to_all(t, ("x", "y"), 0, 0, tiled=True)
    w = weight_grad.reshape(BA, 2, BG).transpose(1, 0, 2)
    w_far = swap_zh(w)
    u = turn(layer_inputs, BA, lambda b: b, 2)
    w = jnp.concatenate([w, w_far], axis=0)
    t, w, u = tie(t, w, u)
    w1, w3 = along_y(w, 1), along_y(w, 3)
    mine, other = gram(zc, t)
    mine, other, u = tie(mine, other, u)
    u = lax.all_to_all(u, ("x", "y"), 0, 0, tiled=True)
    own, part = sum_over_copies(mine, other)
    m, t1 = first_inverse(zc, own, part)
    m, t1, w1, w3, u = tie(m, t1, w1, w3, u)
    w2 = [along_y(w1[:2], 1), along_y(w3[2:], 3)]
    q1 = near(t1)
    act = small_inverse(small_sum(small_gram(u), c))
    m, q1, act, *w2 = tie(m, q1, act, *w2)
    one = far(q1)
    q1_other = swap_core(q1)
    act = move(act, ("zl", "c", "y"), lambda zl, c, y: (y >> 1, y & 1, 2 * zl + c))
    t2 = second_inverse(m)
    t2, act, q1_other, one[1], one[3] = tie(t2, act, q1_other, one[1], one[3])
    two = far(near(t2))
    left = left_rows(at, act, [w, w1, *w2, w3])
    one_other = [q1_other] + [swap_core(v) for v in one[1:]]
    return apply(at, left, one, one_other, two)


def solution(mesh):
    fine = Mesh(np.asarray(mesh.devices).reshape(tuple(SIZES.values())), tuple(SIZES))
    dp, owner = ("x", "zl", "c"), ("y", "zh")
    return jax.shard_map(
        shards,
        mesh=fine,
        in_specs=(P(dp + owner, None), P(dp + owner, None), P(dp, owner)),
        out_specs=P(dp, None),
        check_vma=False,
    )
```

```python
import functools
import jax, jax.numpy as jnp
from jax import lax
from jax.experimental import pallas as pl
from jax.experimental.pallas import tpu as pltpu
f32=jnp.float32; bf16=jnp.bfloat16
NB=128

def split3(x):
    h=x.astype(bf16); r=x-h.astype(f32)
    m=r.astype(bf16); l=(r-m.astype(f32)).astype(bf16)
    return h,m,l

def bc(x,j):
    return jnp.broadcast_to(x[j:j+1,:],(8,128))

def tree(v):
    while len(v)>1:
        v=[a+b for a,b in zip(v[::2],v[1::2])]+([v[-1]] if len(v)%2 else [])
    return v[0]

def eliminate(chains):
    lane=lax.broadcasted_iota(jnp.int32,(8,128),1); sub=lax.broadcasted_iota(jnp.int32,(8,128),0)
    outs=[[] for _ in chains]
    for g in range(16):
        lo=8*g
        ing=(lane>=lo)&(lane<lo+8)
        eye=jnp.where(lane-lo==sub,1.0,0.0).astype(f32)
        st=[]
        for rows in chains:
            R=rows[g]
            B=[jnp.broadcast_to(R[:,lo+j:lo+j+1],(8,128)) for j in range(8)]
            S={(i,q):bc(B[q],i) for q in range(8) for i in range(q+1)}
            st.append([jnp.where(ing,eye,R),B,jnp.zeros((8,128),f32),S])
        for j in range(8):
            for s_ in st:
                R,B,U,S=s_
                p=S[j,j]
                r0=pl.reciprocal(p,approx=True)
                e=2.0-p*r0
                inv=r0*e
                for i in range(j+1,8):
                    for q in range(i,8):
                        S[i,q]=S[i,q]-((S[j,i]*S[j,q])*r0)*e
                rs=lax.rsqrt(p)
                rs=rs*(1.5-0.5*p*rs*rs)
                b=bc(R,j)
                U=jnp.where(sub==j,b*rs,U)
                m=b*inv
                R=jnp.where(sub==j,m,R-B[j]*m)
                for q in range(j+1,8):
                    s=S[j,q]*inv
                    B[q]=jnp.where(sub==j,s,B[q]-B[j]*s)
                s_[0]=R; s_[2]=U
        for ci,(rows,s_) in enumerate(zip(chains,st)):
            W=s_[0]; outs[ci].append(s_[2])
            w=[bc(W,j) for j in range(8)]
            for i in range(g+1,16):
                a=rows[i]
                rows[i]=jnp.where(ing,0.0,a)-tree([jnp.broadcast_to(a[:,lo+j:lo+j+1],(8,128))*w[j] for j in range(8)])
    return outs

def dot(a,b,ca,cb):
    return lax.dot_general(a,b,(((ca,),(cb,)),((),())),preferred_element_type=f32)

def load_diag(M,k,off=0):
    cols=pl.ds(pl.multiple_of(k*NB,NB),NB)
    return [M[pl.ds(pl.multiple_of((k-off)*NB+8*i,8),8),cols] for i in range(16)]

def store_lower(LD,rows):
    lane=lax.broadcasted_iota(jnp.int32,(8,128),1); sub=lax.broadcasted_iota(jnp.int32,(8,128),0)
    for i,u in enumerate(rows):
        LD[8*i:8*i+8,:]=jnp.where(lane<=sub+8*i,u,0.0)

def eye(n):
    return jnp.where(lax.broadcasted_iota(jnp.int32,(n,n),0)==lax.broadcasted_iota(jnp.int32,(n,n),1),1.0,0.0).astype(f32)

def panel(M,LD,k,n,off=0):
    nb=n//NB; c0=k*NB; r0=c0-off*NB
    M[r0:r0+NB,c0:c0+NB]=eye(NB)
    lh,lm,ll=split3(LD[...])
    mh,mm,ml=split3(M[r0:r0+NB,:])
    hm=jnp.concatenate([mh,mm],0); lhh=jnp.concatenate([ml,mh],0)
    U=dot(jnp.concatenate([lh,lh],1),hm,1,0)+dot(jnp.concatenate([lm,lm],1),hm,1,0)+dot(jnp.concatenate([lh,ll],1),lhh,1,0)
    M[r0:r0+NB,:]=U
    if k+1<nb:
        h,m,l=split3(U)
        c,r=c0+NB,r0+NB
        hm=jnp.concatenate([h,m],0); lhh=jnp.concatenate([l,h],0)
        ht,mt,lt=h[:,c:].T,m[:,c:].T,l[:,c:].T
        S=dot(jnp.concatenate([ht,ht],1),hm,1,0)+dot(jnp.concatenate([mt,mt],1),hm,1,0)+dot(jnp.concatenate([ht,lt],1),lhh,1,0)
        M[r:,c0:c]=jnp.zeros((n-c,NB),f32)
        M[r:,:]=M[r:,:]-S

def each(k,ks,f):
    for kk in ks:
        @pl.when(k==kk)
        def _(): f(kk)

def steps(M,LD,n,ks,off=0,Ma=None,LDa=None,na=0):
    def body(k,_):
        blocks=[load_diag(M,k,off)]
        if Ma is not None: blocks.append(load_diag(Ma,k-ks[0]))
        out=eliminate(blocks)
        store_lower(LD,out[0])
        if Ma is not None: store_lower(LDa,out[1])
        def both(kk):
            panel(M,LD,kk,n,off)
            if Ma is not None: panel(Ma,LDa,kk-ks[0],na)
        each(k,ks,both)
        return 0
    lax.fori_loop(ks[0],ks[-1]+1,body,0)


import itertools
import math
import numpy as np
from jax.sharding import Mesh, PartitionSpec as P

BA = 320
BG = 864
GP = 896
AP = 384
TOKENS = 16384.0
DAMPING = 0.1
SIZES = dict(x=4, zl=2, c=2, y=4, zh=2)
GB = [(i, j) for i in range(GP // NB) for j in range(i, GP // NB)]
AB = [(i, j) for i in range(AP // NB) for j in range(i, AP // NB)]
ROWS = len(GB) * NB
CHUNK = ROWS // 8
VMEM = pltpu.CompilerParams(vmem_limit_bytes=56 << 20)


def move(a, names, target):
    dims = [SIZES[n] for n in names]
    pairs = []
    for at in itertools.product(*map(range, dims)):
        to = target(*at)
        pairs.append((int(np.ravel_multi_index(at, dims)), int(np.ravel_multi_index(to, dims))))
    return lax.ppermute(a, names, pairs)


def along_z(a, d):
    def target(zl, zh):
        z = (2 * zh + zl + d) % 4
        return z % 2, z // 2
    return move(a, ("zl", "zh"), target)


def along_y(a, d):
    return move(a, ("y",), lambda y: ((y + d) % 4,))


def swap_core(a):
    return move(a, ("c",), lambda c: (1 - c,))


def swap_zh(a):
    return move(a, ("zh",), lambda h: (1 - h,))


def in_plane(a, d, first):
    def target(x, c, y):
        return ((x + d) % 4, c, y) if (c == 0) == first else (x, c, (y + d) % 4)
    return move(a, ("x", "c", "y"), target)


def cost(us):
    return pl.CostEstimate(flops=int(us * 1e9), bytes_accessed=1 << 20, transcendentals=0)


def turn_kernel(size, slot, g_ref, o_ref):
    for t in range(g_ref.shape[1] // NB):
        tile = g_ref[:, t * NB:(t + 1) * NB].T
        at, end = t * NB, (t + 1) * NB
        while at < end:
            b = at // size
            stop = min(end, (b + 1) * size)
            o_ref[slot(b), at - b * size:stop - b * size, :] = tile[at - t * NB:stop - t * NB, :]
            at = stop


def turn(g, size, slot, us):
    return pl.pallas_call(
        functools.partial(turn_kernel, size, slot),
        out_shape=jax.ShapeDtypeStruct((16, size, NB), bf16),
        compiler_params=VMEM,
        cost_estimate=cost(us),
    )(g)


def products(t_ref, s_ref, p_ref, size, n, blocks):
    if size < n:
        s_ref[size:, :] = jnp.zeros((n - size, 16 * NB), bf16)
    for s in range(16):
        s_ref[:size, s * NB:(s + 1) * NB] = t_ref[s]
    for r0 in range(0, n, 2 * NB):
        rows = min(2 * NB, n - r0)
        d = dot(s_ref[r0:r0 + rows, :], s_ref[r0:, :], 1, 1)
        for k, (i, j) in enumerate(blocks):
            if r0 <= i * NB < r0 + rows:
                p_ref[k * NB:(k + 1) * NB, :] = d[i * NB - r0:(i + 1) * NB - r0, j * NB - r0:(j + 1) * NB - r0]


def gram_kernel(at_ref, t_ref, mine_ref, other_ref, s_ref, p_ref):
    z, c = at_ref[0], at_ref[1]
    products(t_ref, s_ref, p_ref, BG, GP, GB)
    for q in range(4):
        d = lax.rem(q - z + 4, 4)
        rows = pl.ds(pl.multiple_of(d * CHUNK, 8), CHUNK)
        first, second = p_ref[q * CHUNK:(q + 1) * CHUNK, :], p_ref[(4 + q) * CHUNK:(5 + q) * CHUNK, :]
        mine_ref[rows, :] = jnp.where(c == 0, first, second)
        other_ref[rows, :] = jnp.where(c == 0, second, first)


def gram(at, t):
    half = jax.ShapeDtypeStruct((4 * CHUNK, NB), f32)
    return pl.pallas_call(
        gram_kernel,
        out_shape=(half, half),
        in_specs=[pl.BlockSpec(memory_space=pltpu.SMEM), pl.BlockSpec(memory_space=pltpu.VMEM)],
        scratch_shapes=[pltpu.VMEM((GP, 16 * NB), bf16), pltpu.VMEM((ROWS, NB), f32)],
        compiler_params=VMEM,
        cost_estimate=cost(8),
    )(at, t)


def small_gram_kernel(t_ref, p_ref, s_ref):
    products(t_ref, s_ref, p_ref, BA, AP, AB)


def small_gram(t):
    return pl.pallas_call(
        small_gram_kernel,
        out_shape=jax.ShapeDtypeStruct((len(AB) * NB, NB), f32),
        scratch_shapes=[pltpu.VMEM((AP, 16 * NB), bf16)],
        compiler_params=VMEM,
        cost_estimate=cost(3),
    )(t)


def sum_over_copies(mine, other):
    h = mine + swap_core(other)
    part = [h[d * CHUNK:(d + 1) * CHUNK] for d in range(4)]
    got = [along_z(part[d], d) for d in (1, 2, 3)]
    s = part[0] + got[0] + got[1] + got[2]
    own = jnp.concatenate([s] + [along_z(s, d) for d in (1, 2, 3)], axis=0)
    return own, swap_core(own)


def small_sum(p, c):
    half = len(AB) * NB // 2
    first, second = p[:half], p[half:]
    h = jnp.where(c == 0, first, second) + swap_core(jnp.where(c == 0, second, first))
    got = [along_z(h, d) for d in (1, 2, 3)]
    s = (h + got[1]) + (got[0] + got[2])
    o = swap_core(s)
    return jnp.concatenate([jnp.where(c == 0, s, o), jnp.where(c == 0, o, s)], axis=0)


def unpack(M, n, blocks, p_ref):
    M[...] = jnp.zeros((n, n), f32)
    for k, (i, j) in enumerate(blocks):
        block = p_ref[k * NB:(k + 1) * NB, :] / TOKENS
        if i == j:
            block = block + DAMPING * eye(NB)
        M[i * NB:(i + 1) * NB, j * NB:(j + 1) * NB] = block


def lower():
    return lax.broadcasted_iota(jnp.int32, (NB, NB), 0) >= lax.broadcasted_iota(jnp.int32, (NB, NB), 1)


TOP = 512
REST = BG - TOP
PACK = 128 + 256 + REST


def tidy(M, n):
    for i in range(n // NB):
        M[i * NB:(i + 1) * NB, i * NB:(i + 1) * NB] = jnp.where(lower(), M[i * NB:(i + 1) * NB, i * NB:(i + 1) * NB], 0.0)


def first_kernel(at_ref, own_ref, part_ref, m_ref, t_ref, p_ref, M, LD, s_ref):
    z, c = at_ref[0], at_ref[1]
    for d in range(4):
        q = lax.rem(z - d + 4, 4)
        p_ref[pl.ds(pl.multiple_of((4 * c + q) * CHUNK, 8), CHUNK), :] = own_ref[d * CHUNK:(d + 1) * CHUNK, :]
        p_ref[pl.ds(pl.multiple_of((4 * (1 - c) + q) * CHUNK, 8), CHUNK), :] = part_ref[d * CHUNK:(d + 1) * CHUNK, :]
    unpack(M, GP, GB, p_ref)
    steps(M, LD, GP, range(4))
    m_ref[...] = M[TOP:, TOP:]
    tidy(M, TOP)
    for i in (0, 2):
        M[i * NB:(i + 1) * NB, (i + 1) * NB:(i + 2) * NB] = jnp.zeros((NB, NB), f32)
    s_ref[0:128, 0:256] = M[0:128, 0:256].astype(bf16)
    s_ref[0:128, 256:512] = M[128:256, 0:256].astype(bf16)
    s_ref[128:384, :] = M[256:512, :TOP].astype(bf16)
    s_ref[384:, :] = M[TOP:BG, :TOP].astype(bf16)
    t_ref[...] = s_ref[pl.ds(pl.multiple_of(c * (PACK // 2), 16), PACK // 2), :]


def first_inverse(at, own, part):
    return pl.pallas_call(
        first_kernel,
        out_shape=(jax.ShapeDtypeStruct((AP, AP), f32), jax.ShapeDtypeStruct((PACK // 2, TOP), bf16)),
        in_specs=[pl.BlockSpec(memory_space=pltpu.SMEM)] + [pl.BlockSpec(memory_space=pltpu.VMEM)] * 2,
        scratch_shapes=[
            pltpu.VMEM((ROWS, NB), f32),
            pltpu.VMEM((GP, GP), f32),
            pltpu.VMEM((NB, NB), f32),
            pltpu.VMEM((PACK, TOP), bf16),
        ],
        compiler_params=VMEM,
        cost_estimate=cost(2),
    )(at, own, part)


def second_kernel(m_in, t_ref, M, LD):
    M[...] = m_in[...]
    steps(M, LD, AP, range(3))
    tidy(M, AP)
    at = 0
    for i in range(3):
        rows = min(NB, REST - i * NB)
        for j in range(i + 1):
            t_ref[at:at + rows, :] = M[i * NB:i * NB + rows, j * NB:(j + 1) * NB].astype(bf16)
            at += rows


LAST = 3 * NB + 3 * (REST - 2 * NB)


def second_inverse(m):
    return pl.pallas_call(
        second_kernel,
        out_shape=jax.ShapeDtypeStruct((LAST, NB), bf16),
        scratch_shapes=[pltpu.VMEM((AP, AP), f32), pltpu.VMEM((NB, NB), f32)],
        compiler_params=VMEM,
        cost_estimate=cost(1),
    )(m)


def small_inverse_kernel(a_in, inv_ref, M, LD):
    unpack(M, AP, AB, a_in)
    steps(M, LD, AP, range(3))
    tidy(M, AP)
    n = AP // NB
    for i in range(n):
        for j in range(i + 1, n):
            M[i * NB:(i + 1) * NB, j * NB:(j + 1) * NB] = jnp.zeros((NB, NB), f32)
    L = M[:BA, :BA]
    inv_ref[...] = lax.dot_general(
        L, L, (((0,), (0,)), ((), ())), precision=lax.Precision.HIGHEST, preferred_element_type=f32
    ).astype(bf16)


def small_inverse(a):
    return pl.pallas_call(
        small_inverse_kernel,
        out_shape=jax.ShapeDtypeStruct((BA, BA), bf16),
        scratch_shapes=[pltpu.VMEM((AP, AP), f32), pltpu.VMEM((NB, NB), f32)],
        compiler_params=VMEM,
        cost_estimate=cost(1),
    )(a)


def near(t):
    return jnp.stack([t] + [in_plane(t, d, True) for d in (1, 2, 3)])


def far(q):
    return [q] + [in_plane(q, d, False) for d in (1, 2, 3)]


def left_kernel(at_ref, act_ref, *refs):
    w, (o_ref, wv, sem) = refs[0:5], refs[5:]
    d, zh = pl.program_id(0), at_ref[2]

    def copies(k):
        if k == 2:
            return [
                pltpu.make_async_copy(w[2], wv.at[2, 0:2], sem.at[2]),
                pltpu.make_async_copy(w[3], wv.at[2, 2:4], sem.at[4]),
            ]
        return [pltpu.make_async_copy(w[(0, 1, None, 4)[k]], wv.at[k], sem.at[k])]

    @pl.when(d == 0)
    def _():
        for k in range(4):
            for m in copies(k):
                m.start()

    for k in range(4):
        @pl.when(d == k)
        def _():
            for m in copies(k):
                m.wait()
    for xb in range(4):
        zb, h = xb // 2, xb % 2
        o_ref[0, xb] = dot(act_ref[...], wv[d, 2 * jnp.where(zh == zb, 0, 1) + h], 1, 0).astype(bf16)


def left_rows(at, act, w):
    return pl.pallas_call(
        left_kernel,
        out_shape=jax.ShapeDtypeStruct((4, 4, BA, BG), bf16),
        grid_spec=pltpu.PrefetchScalarGridSpec(
            num_scalar_prefetch=1,
            grid=(4,),
            in_specs=[pl.BlockSpec((BA, BA), lambda d, s: (0, 0))] + [pl.BlockSpec(memory_space=pl.ANY)] * 5,
            out_specs=pl.BlockSpec((1, 4, BA, BG), lambda d, s: (d, 0, 0, 0)),
            scratch_shapes=[pltpu.VMEM((4, 4, BA, BG), bf16), pltpu.SemaphoreType.DMA((5,))],
        ),
        compiler_params=VMEM,
        cost_estimate=cost(8),
    )(at, act, *w)


def apply_kernel(at_ref, l_ref, *refs):
    own, part, two = refs[0:4], refs[4:8], refs[8:12]
    o_ref, va, vb, v, t0, t1, K, sema, semb = refs[12:]
    x, c = at_ref[0], at_ref[3]
    d = pl.program_id(0)
    slot = lax.rem(d, 2)

    def fetch(k):
        for core in range(2):
            @pl.when(c == core)
            def _():
                first, second = (own, part) if core == 0 else (part, own)
                pltpu.make_async_copy(first[k], va.at[k % 2], sema.at[k % 2]).start()
                for q in range(4):
                    pltpu.make_async_copy(second[q].at[k], vb.at[k % 2, q], semb.at[k % 2, q]).start()

    @pl.when(d == 0)
    def _():
        fetch(0)
        K[...] = jnp.zeros(K.shape, bf16)
        for k in range(4):
            v[k] = two[k][...]

    for k in range(3):
        @pl.when(d == k)
        def _():
            fetch(k + 1)

    pltpu.make_async_copy(own[0], va.at[slot], sema.at[slot]).wait()
    for q in range(4):
        pltpu.make_async_copy(own[0].at[0], vb.at[slot, q], semb.at[slot, q]).wait()

    half = PACK // 2
    for xb in range(4):
        dx = lax.rem(x - xb + 4, 4)
        s = xb % 2
        t0[s, 0:128, :] = va[slot, dx, 0:128, 0:256]
        t0[s, 128:256, :] = va[slot, dx, 0:128, 256:512]
        t1[s, 0:half - 128, :] = va[slot, dx, 128:half, :]
        t1[s, half - 128:256, :] = vb[slot, dx, 0:384 - half, :]
        k = v.at[jnp.where(c == 0, d, dx), jnp.where(c == 0, dx, d)]
        at = 0
        for i in range(3):
            rows = min(NB, REST - i * NB)
            for j in range(i + 1):
                K[s, i * NB:i * NB + rows, j * NB:(j + 1) * NB] = k[at:at + rows, :]
                at += rows
        e = vb[slot, dx, 384 - half:half, :]
        kk = K[s][:, :REST]
        left = l_ref[0, xb]
        l0 = left[:, :TOP]
        u = (left[:, TOP:].astype(f32) + dot(l0, e, 1, 1)).astype(bf16)
        y0 = dot(l0[:, :256], t0[s], 1, 1).astype(bf16)
        y1 = dot(l0, t1[s], 1, 1).astype(bf16)
        g = dot(dot(u, kk, 1, 1).astype(bf16), kk, 1, 0).astype(bf16)
        r = dot(y1, t1[s], 1, 0) + dot(g, e, 1, 0)
        o_ref[:, xb * BG:xb * BG + 256] = (r[:, :256] + dot(y0, t0[s], 1, 0)).astype(bf16)
        o_ref[:, xb * BG + 256:xb * BG + TOP] = r[:, 256:].astype(bf16)
        o_ref[:, xb * BG + TOP:(xb + 1) * BG] = g


def apply(at, left, own, part, two):
    any_space = pl.BlockSpec(memory_space=pl.ANY)
    return pl.pallas_call(
        apply_kernel,
        out_shape=jax.ShapeDtypeStruct((BA, 16 * BG), bf16),
        grid_spec=pltpu.PrefetchScalarGridSpec(
            num_scalar_prefetch=1,
            grid=(4,),
            in_specs=[pl.BlockSpec((1, 4, BA, BG), lambda d, s: (d, 0, 0, 0))]
            + [any_space] * 8
            + [pl.BlockSpec((4, LAST, NB), lambda d, s: (0, 0, 0))] * 4,
            out_specs=pl.BlockSpec((BA, 4 * BG), lambda d, s: (0, lax.rem(s[1] - d + 4, 4))),
            scratch_shapes=[
                pltpu.VMEM((2, 4, PACK // 2, TOP), bf16),
                pltpu.VMEM((2, 4, PACK // 2, TOP), bf16),
                pltpu.VMEM((4, 4, LAST, NB), bf16),
                pltpu.VMEM((2, 256, 256), bf16),
                pltpu.VMEM((2, 256, TOP), bf16),
                pltpu.VMEM((2, REST, AP), bf16),
                pltpu.SemaphoreType.DMA((2,)),
                pltpu.SemaphoreType.DMA((2, 4)),
            ],
        ),
        compiler_params=VMEM,
        cost_estimate=cost(25),
    )(at, left, *own, *part, *two)


def tie(*arrays):
    return lax.optimization_barrier(arrays)


def shards(layer_inputs, output_grads, weight_grad):
    x, y, zh, zl, c = (lax.axis_index(n) for n in ("x", "y", "zh", "zl", "c"))
    zc = jnp.stack([2 * zh + zl, c]).astype(jnp.int32)
    at = jnp.stack([x, y, zh, c]).astype(jnp.int32)

    t = turn(output_grads, BG, lambda b: 4 * (b % 4) + b // 4, 5)
    t, weight_grad, layer_inputs = tie(t, weight_grad, layer_inputs)
    t = lax.all_to_all(t, ("x", "y"), 0, 0, tiled=True)
    w = weight_grad.reshape(BA, 2, BG).transpose(1, 0, 2)
    w_far = swap_zh(w)
    u = turn(layer_inputs, BA, lambda b: b, 2)
    w = jnp.concatenate([w, w_far], axis=0)
    t, w, u = tie(t, w, u)
    w1, w3 = along_y(w, 1), along_y(w, 3)
    mine, other = gram(zc, t)
    mine, other, u = tie(mine, other, u)
    u = lax.all_to_all(u, ("x", "y"), 0, 0, tiled=True)
    own, part = sum_over_copies(mine, other)
    m, t1 = first_inverse(zc, own, part)
    m, t1, w1, w3, u = tie(m, t1, w1, w3, u)
    w2 = [along_y(w1[:2], 1), along_y(w3[2:], 3)]
    q1 = near(t1)
    a = small_gram(u)
    m, q1, a, *w2 = tie(m, q1, a, *w2)
    one = far(q1)
    q1_other = swap_core(q1)
    t2 = second_inverse(m)
    t2, a, q1_other, one[1], one[3] = tie(t2, a, q1_other, one[1], one[3])
    q2 = near(t2)
    a = small_sum(a, c)
    q2, a = tie(q2, a)
    two = far(q2)
    act = small_inverse(a)
    act, one[2], *two = tie(act, one[2], *two)
    act = move(act, ("zl", "c", "y"), lambda zl, c, y: (y >> 1, y & 1, 2 * zl + c))
    left = left_rows(at, act, [w, w1, *w2, w3])
    one_other = [q1_other] + [swap_core(v) for v in one[1:]]
    return apply(at, left, one, one_other, two)


def solution(mesh):
    fine = Mesh(np.asarray(mesh.devices).reshape(tuple(SIZES.values())), tuple(SIZES))
    dp, owner = ("x", "zl", "c"), ("y", "zh")
    return jax.shard_map(
        shards,
        mesh=fine,
        in_specs=(P(dp + owner, None), P(dp + owner, None), P(dp, owner)),
        out_specs=P(dp, None),
        check_vma=False,
    )
```

```python
import functools
import jax, jax.numpy as jnp
from jax import lax
from jax.experimental import pallas as pl
from jax.experimental.pallas import tpu as pltpu
f32=jnp.float32; bf16=jnp.bfloat16
NB=128

def split3(x):
    h=x.astype(bf16); r=x-h.astype(f32)
    m=r.astype(bf16); l=(r-m.astype(f32)).astype(bf16)
    return h,m,l

def bc(x,j):
    return jnp.broadcast_to(x[j:j+1,:],(8,128))

def tree(v):
    while len(v)>1:
        v=[a+b for a,b in zip(v[::2],v[1::2])]+([v[-1]] if len(v)%2 else [])
    return v[0]

def eliminate(chains):
    lane=lax.broadcasted_iota(jnp.int32,(8,128),1); sub=lax.broadcasted_iota(jnp.int32,(8,128),0)
    outs=[[] for _ in chains]
    for g in range(16):
        lo=8*g
        ing=(lane>=lo)&(lane<lo+8)
        eye=jnp.where(lane-lo==sub,1.0,0.0).astype(f32)
        st=[]
        for rows in chains:
            R=rows[g]
            B=[jnp.broadcast_to(R[:,lo+j:lo+j+1],(8,128)) for j in range(8)]
            S={(i,q):bc(B[q],i) for q in range(8) for i in range(q+1)}
            st.append([jnp.where(ing,eye,R),B,jnp.zeros((8,128),f32),S])
        for j in range(8):
            for s_ in st:
                R,B,U,S=s_
                p=S[j,j]
                r0=pl.reciprocal(p,approx=True)
                e=2.0-p*r0
                inv=r0*e
                for i in range(j+1,8):
                    for q in range(i,8):
                        S[i,q]=S[i,q]-((S[j,i]*S[j,q])*r0)*e
                rs=lax.rsqrt(p)
                rs=rs*(1.5-0.5*p*rs*rs)
                b=bc(R,j)
                U=jnp.where(sub==j,b*rs,U)
                m=b*inv
                R=jnp.where(sub==j,m,R-B[j]*m)
                for q in range(j+1,8):
                    s=S[j,q]*inv
                    B[q]=jnp.where(sub==j,s,B[q]-B[j]*s)
                s_[0]=R; s_[2]=U
        for ci,(rows,s_) in enumerate(zip(chains,st)):
            W=s_[0]; outs[ci].append(s_[2])
            w=[bc(W,j) for j in range(8)]
            for i in range(g+1,16):
                a=rows[i]
                rows[i]=jnp.where(ing,0.0,a)-tree([jnp.broadcast_to(a[:,lo+j:lo+j+1],(8,128))*w[j] for j in range(8)])
    return outs

def dot(a,b,ca,cb):
    return lax.dot_general(a,b,(((ca,),(cb,)),((),())),preferred_element_type=f32)

def load_diag(M,k,off=0):
    cols=pl.ds(pl.multiple_of(k*NB,NB),NB)
    return [M[pl.ds(pl.multiple_of((k-off)*NB+8*i,8),8),cols] for i in range(16)]

def store_lower(LD,rows):
    lane=lax.broadcasted_iota(jnp.int32,(8,128),1); sub=lax.broadcasted_iota(jnp.int32,(8,128),0)
    for i,u in enumerate(rows):
        LD[8*i:8*i+8,:]=jnp.where(lane<=sub+8*i,u,0.0)

def eye(n):
    return jnp.where(lax.broadcasted_iota(jnp.int32,(n,n),0)==lax.broadcasted_iota(jnp.int32,(n,n),1),1.0,0.0).astype(f32)

def panel(M,LD,k,n,off=0):
    nb=n//NB; c0=k*NB; r0=c0-off*NB
    M[r0:r0+NB,c0:c0+NB]=eye(NB)
    lh,lm,ll=split3(LD[...])
    mh,mm,ml=split3(M[r0:r0+NB,:])
    hm=jnp.concatenate([mh,mm],0); lhh=jnp.concatenate([ml,mh],0)
    U=dot(jnp.concatenate([lh,lh],1),hm,1,0)+dot(jnp.concatenate([lm,lm],1),hm,1,0)+dot(jnp.concatenate([lh,ll],1),lhh,1,0)
    M[r0:r0+NB,:]=U
    if k+1<nb:
        h,m,l=split3(U)
        c,r=c0+NB,r0+NB
        hm=jnp.concatenate([h,m],0); lhh=jnp.concatenate([l,h],0)
        ht,mt,lt=h[:,c:].T,m[:,c:].T,l[:,c:].T
        S=dot(jnp.concatenate([ht,ht],1),hm,1,0)+dot(jnp.concatenate([mt,mt],1),hm,1,0)+dot(jnp.concatenate([ht,lt],1),lhh,1,0)
        M[r:,c0:c]=jnp.zeros((n-c,NB),f32)
        M[r:,:]=M[r:,:]-S

def each(k,ks,f):
    for kk in ks:
        @pl.when(k==kk)
        def _(): f(kk)

def steps(M,LD,n,ks,off=0,Ma=None,LDa=None,na=0):
    def body(k,_):
        blocks=[load_diag(M,k,off)]
        if Ma is not None: blocks.append(load_diag(Ma,k-ks[0]))
        out=eliminate(blocks)
        store_lower(LD,out[0])
        if Ma is not None: store_lower(LDa,out[1])
        def both(kk):
            panel(M,LD,kk,n,off)
            if Ma is not None: panel(Ma,LDa,kk-ks[0],na)
        each(k,ks,both)
        return 0
    lax.fori_loop(ks[0],ks[-1]+1,body,0)


import itertools
import math
import numpy as np
from jax.sharding import Mesh, PartitionSpec as P

BA = 320
BG = 864
GP = 896
AP = 384
TOKENS = 16384.0
DAMPING = 0.1
SIZES = dict(x=4, zl=2, c=2, y=4, zh=2)
GB = [(i, j) for i in range(GP // NB) for j in range(i, GP // NB)]
AB = [(i, j) for i in range(AP // NB) for j in range(i, AP // NB)]
ROWS = len(GB) * NB
CHUNK = ROWS // 8
VMEM = pltpu.CompilerParams(vmem_limit_bytes=56 << 20)


def move(a, names, target):
    dims = [SIZES[n] for n in names]
    pairs = []
    for at in itertools.product(*map(range, dims)):
        to = target(*at)
        pairs.append((int(np.ravel_multi_index(at, dims)), int(np.ravel_multi_index(to, dims))))
    return lax.ppermute(a, names, pairs)


def along_z(a, d):
    def target(zl, zh):
        z = (2 * zh + zl + d) % 4
        return z % 2, z // 2
    return move(a, ("zl", "zh"), target)


def along_y(a, d):
    return move(a, ("y",), lambda y: ((y + d) % 4,))


def swap_core(a):
    return move(a, ("c",), lambda c: (1 - c,))


def swap_zh(a):
    return move(a, ("zh",), lambda h: (1 - h,))


def in_plane(a, d, first):
    def target(x, c, y):
        return ((x + d) % 4, c, y) if (c == 0) == first else (x, c, (y + d) % 4)
    return move(a, ("x", "c", "y"), target)


def cost(us):
    return pl.CostEstimate(flops=int(us * 1e9), bytes_accessed=1 << 20, transcendentals=0)


def turn_kernel(size, slot, g_ref, o_ref):
    for t in range(g_ref.shape[1] // NB):
        tile = g_ref[:, t * NB:(t + 1) * NB].T
        at, end = t * NB, (t + 1) * NB
        while at < end:
            b = at // size
            stop = min(end, (b + 1) * size)
            o_ref[slot(b), at - b * size:stop - b * size, :] = tile[at - t * NB:stop - t * NB, :]
            at = stop


def turn(g, size, slot, us):
    return pl.pallas_call(
        functools.partial(turn_kernel, size, slot),
        out_shape=jax.ShapeDtypeStruct((16, size, NB), bf16),
        compiler_params=VMEM,
        cost_estimate=cost(us),
    )(g)


def products(t_ref, s_ref, p_ref, size, n, blocks):
    if size < n:
        s_ref[size:, :] = jnp.zeros((n - size, 16 * NB), bf16)
    for s in range(16):
        s_ref[:size, s * NB:(s + 1) * NB] = t_ref[s]
    for r0 in range(0, n, 2 * NB):
        rows = min(2 * NB, n - r0)
        d = dot(s_ref[r0:r0 + rows, :], s_ref[r0:, :], 1, 1)
        for k, (i, j) in enumerate(blocks):
            if r0 <= i * NB < r0 + rows:
                p_ref[k * NB:(k + 1) * NB, :] = d[i * NB - r0:(i + 1) * NB - r0, j * NB - r0:(j + 1) * NB - r0]


def gram_kernel(at_ref, t_ref, mine_ref, other_ref, s_ref, p_ref):
    z, c = at_ref[0], at_ref[1]
    products(t_ref, s_ref, p_ref, BG, GP, GB)
    for q in range(4):
        d = lax.rem(q - z + 4, 4)
        rows = pl.ds(pl.multiple_of(d * CHUNK, 8), CHUNK)
        first, second = p_ref[q * CHUNK:(q + 1) * CHUNK, :], p_ref[(4 + q) * CHUNK:(5 + q) * CHUNK, :]
        mine_ref[rows, :] = jnp.where(c == 0, first, second)
        other_ref[rows, :] = jnp.where(c == 0, second, first)


def gram(at, t):
    half = jax.ShapeDtypeStruct((4 * CHUNK, NB), f32)
    return pl.pallas_call(
        gram_kernel,
        out_shape=(half, half),
        in_specs=[pl.BlockSpec(memory_space=pltpu.SMEM), pl.BlockSpec(memory_space=pltpu.VMEM)],
        scratch_shapes=[pltpu.VMEM((GP, 16 * NB), bf16), pltpu.VMEM((ROWS, NB), f32)],
        compiler_params=VMEM,
        cost_estimate=cost(8),
    )(at, t)


def small_gram_kernel(t_ref, p_ref, s_ref):
    products(t_ref, s_ref, p_ref, BA, AP, AB)


def small_gram(t):
    return pl.pallas_call(
        small_gram_kernel,
        out_shape=jax.ShapeDtypeStruct((len(AB) * NB, NB), f32),
        scratch_shapes=[pltpu.VMEM((AP, 16 * NB), bf16)],
        compiler_params=VMEM,
        cost_estimate=cost(3),
    )(t)


def sum_over_copies(mine, other):
    h = mine + swap_core(other)
    part = [h[d * CHUNK:(d + 1) * CHUNK] for d in range(4)]
    got = [along_z(part[d], d) for d in (1, 2, 3)]
    s = part[0] + got[0] + got[1] + got[2]
    own = jnp.concatenate([s] + [along_z(s, d) for d in (1, 2, 3)], axis=0)
    return own, swap_core(own)


def small_sum(p, c):
    half = len(AB) * NB // 2
    first, second = p[:half], p[half:]
    h = jnp.where(c == 0, first, second) + swap_core(jnp.where(c == 0, second, first))
    got = [along_z(h, d) for d in (1, 2, 3)]
    s = (h + got[1]) + (got[0] + got[2])
    o = swap_core(s)
    return jnp.concatenate([jnp.where(c == 0, s, o), jnp.where(c == 0, o, s)], axis=0)


def unpack(M, n, blocks, p_ref):
    M[...] = jnp.zeros((n, n), f32)
    for k, (i, j) in enumerate(blocks):
        block = p_ref[k * NB:(k + 1) * NB, :] / TOKENS
        if i == j:
            block = block + DAMPING * eye(NB)
        M[i * NB:(i + 1) * NB, j * NB:(j + 1) * NB] = block


def lower():
    return lax.broadcasted_iota(jnp.int32, (NB, NB), 0) >= lax.broadcasted_iota(jnp.int32, (NB, NB), 1)


TOP = 512
REST = BG - TOP
PACK = 128 + 256 + REST


def tidy(M, n):
    for i in range(n // NB):
        M[i * NB:(i + 1) * NB, i * NB:(i + 1) * NB] = jnp.where(lower(), M[i * NB:(i + 1) * NB, i * NB:(i + 1) * NB], 0.0)


def first_kernel(at_ref, own_ref, part_ref, m_ref, t_ref, p_ref, M, LD, s_ref):
    z, c = at_ref[0], at_ref[1]
    for d in range(4):
        q = lax.rem(z - d + 4, 4)
        p_ref[pl.ds(pl.multiple_of((4 * c + q) * CHUNK, 8), CHUNK), :] = own_ref[d * CHUNK:(d + 1) * CHUNK, :]
        p_ref[pl.ds(pl.multiple_of((4 * (1 - c) + q) * CHUNK, 8), CHUNK), :] = part_ref[d * CHUNK:(d + 1) * CHUNK, :]
    unpack(M, GP, GB, p_ref)
    steps(M, LD, GP, range(4))
    m_ref[...] = M[TOP:, TOP:]
    tidy(M, TOP)
    for i in (0, 2):
        M[i * NB:(i + 1) * NB, (i + 1) * NB:(i + 2) * NB] = jnp.zeros((NB, NB), f32)
    s_ref[0:128, 0:256] = M[0:128, 0:256].astype(bf16)
    s_ref[0:128, 256:512] = M[128:256, 0:256].astype(bf16)
    s_ref[128:384, :] = M[256:512, :TOP].astype(bf16)
    s_ref[384:, :] = M[TOP:BG, :TOP].astype(bf16)
    t_ref[...] = s_ref[pl.ds(pl.multiple_of(c * (PACK // 2), 16), PACK // 2), :]


def first_inverse(at, own, part):
    return pl.pallas_call(
        first_kernel,
        out_shape=(jax.ShapeDtypeStruct((AP, AP), f32), jax.ShapeDtypeStruct((PACK // 2, TOP), bf16)),
        in_specs=[pl.BlockSpec(memory_space=pltpu.SMEM)] + [pl.BlockSpec(memory_space=pltpu.VMEM)] * 2,
        scratch_shapes=[
            pltpu.VMEM((ROWS, NB), f32),
            pltpu.VMEM((GP, GP), f32),
            pltpu.VMEM((NB, NB), f32),
            pltpu.VMEM((PACK, TOP), bf16),
        ],
        compiler_params=VMEM,
        cost_estimate=cost(2),
    )(at, own, part)


def second_kernel(m_in, t_ref, M, LD):
    M[...] = m_in[...]
    steps(M, LD, AP, range(3))
    tidy(M, AP)
    at = 0
    for i in range(3):
        rows = min(NB, REST - i * NB)
        for j in range(i + 1):
            t_ref[at:at + rows, :] = M[i * NB:i * NB + rows, j * NB:(j + 1) * NB].astype(bf16)
            at += rows


LAST = 3 * NB + 3 * (REST - 2 * NB)


def second_inverse(m):
    return pl.pallas_call(
        second_kernel,
        out_shape=jax.ShapeDtypeStruct((LAST, NB), bf16),
        scratch_shapes=[pltpu.VMEM((AP, AP), f32), pltpu.VMEM((NB, NB), f32)],
        compiler_params=VMEM,
        cost_estimate=cost(1),
    )(m)


def small_inverse_kernel(a_in, inv_ref, M, LD):
    unpack(M, AP, AB, a_in)
    steps(M, LD, AP, range(3))
    tidy(M, AP)
    n = AP // NB
    for i in range(n):
        for j in range(i + 1, n):
            M[i * NB:(i + 1) * NB, j * NB:(j + 1) * NB] = jnp.zeros((NB, NB), f32)
    L = M[:BA, :BA]
    inv_ref[...] = lax.dot_general(
        L, L, (((0,), (0,)), ((), ())), precision=lax.Precision.HIGHEST, preferred_element_type=f32
    ).astype(bf16)


def small_inverse(a):
    return pl.pallas_call(
        small_inverse_kernel,
        out_shape=jax.ShapeDtypeStruct((BA, BA), bf16),
        scratch_shapes=[pltpu.VMEM((AP, AP), f32), pltpu.VMEM((NB, NB), f32)],
        compiler_params=VMEM,
        cost_estimate=cost(1),
    )(a)


def near(t):
    return jnp.stack([t] + [in_plane(t, d, True) for d in (1, 2, 3)])


def far(q):
    return [q] + [in_plane(q, d, False) for d in (1, 2, 3)]


def left_kernel(at_ref, act_ref, *refs):
    w, (o_ref, wv, sem) = refs[0:5], refs[5:]
    d, zh = pl.program_id(0), at_ref[2]

    def copies(k):
        if k == 2:
            return [
                pltpu.make_async_copy(w[2], wv.at[2, 0:2], sem.at[2]),
                pltpu.make_async_copy(w[3], wv.at[2, 2:4], sem.at[4]),
            ]
        return [pltpu.make_async_copy(w[(0, 1, None, 4)[k]], wv.at[k], sem.at[k])]

    @pl.when(d == 0)
    def _():
        for k in range(4):
            for m in copies(k):
                m.start()

    for k in range(4):
        @pl.when(d == k)
        def _():
            for m in copies(k):
                m.wait()
    for xb in range(4):
        zb, h = xb // 2, xb % 2
        o_ref[0, xb] = dot(act_ref[...], wv[d, 2 * jnp.where(zh == zb, 0, 1) + h], 1, 0).astype(bf16)


def left_rows(at, act, w):
    return pl.pallas_call(
        left_kernel,
        out_shape=jax.ShapeDtypeStruct((4, 4, BA, BG), bf16),
        grid_spec=pltpu.PrefetchScalarGridSpec(
            num_scalar_prefetch=1,
            grid=(4,),
            in_specs=[pl.BlockSpec((BA, BA), lambda d, s: (0, 0))] + [pl.BlockSpec(memory_space=pl.ANY)] * 5,
            out_specs=pl.BlockSpec((1, 4, BA, BG), lambda d, s: (d, 0, 0, 0)),
            scratch_shapes=[pltpu.VMEM((4, 4, BA, BG), bf16), pltpu.SemaphoreType.DMA((5,))],
        ),
        compiler_params=VMEM,
        cost_estimate=cost(8),
    )(at, act, *w)


def apply_kernel(at_ref, l_ref, *refs):
    own, part, two = refs[0:4], refs[4:8], refs[8:12]
    o_ref, va, vb, v, t0, t1, K, sema, semb = refs[12:]
    x, c = at_ref[0], at_ref[3]
    d = pl.program_id(0)
    slot = lax.rem(d, 2)

    def fetch(k):
        for core in range(2):
            @pl.when(c == core)
            def _():
                first, second = (own, part) if core == 0 else (part, own)
                pltpu.make_async_copy(first[k], va.at[k % 2], sema.at[k % 2]).start()
                for q in range(4):
                    pltpu.make_async_copy(second[q].at[k], vb.at[k % 2, q], semb.at[k % 2, q]).start()

    @pl.when(d == 0)
    def _():
        fetch(0)
        K[...] = jnp.zeros(K.shape, bf16)
        for k in range(4):
            v[k] = two[k][...]

    for k in range(3):
        @pl.when(d == k)
        def _():
            fetch(k + 1)

    pltpu.make_async_copy(own[0], va.at[slot], sema.at[slot]).wait()
    for q in range(4):
        pltpu.make_async_copy(own[0].at[0], vb.at[slot, q], semb.at[slot, q]).wait()

    half = PACK // 2
    for xb in range(4):
        dx = lax.rem(x - xb + 4, 4)
        s = xb % 2
        t0[s, 0:128, :] = va[slot, dx, 0:128, 0:256]
        t0[s, 128:256, :] = va[slot, dx, 0:128, 256:512]
        t1[s, 0:half - 128, :] = va[slot, dx, 128:half, :]
        t1[s, half - 128:256, :] = vb[slot, dx, 0:384 - half, :]
        k = v.at[jnp.where(c == 0, d, dx), jnp.where(c == 0, dx, d)]
        at = 0
        for i in range(3):
            rows = min(NB, REST - i * NB)
            for j in range(i + 1):
                K[s, i * NB:i * NB + rows, j * NB:(j + 1) * NB] = k[at:at + rows, :]
                at += rows
        e = vb[slot, dx, 384 - half:half, :]
        kk = K[s][:, :REST]
        left = l_ref[0, xb]
        l0 = left[:, :TOP]
        u = (left[:, TOP:].astype(f32) + dot(l0, e, 1, 1)).astype(bf16)
        y0 = dot(l0[:, :256], t0[s], 1, 1).astype(bf16)
        y1 = dot(l0, t1[s], 1, 1).astype(bf16)
        g = dot(dot(u, kk, 1, 1).astype(bf16), kk, 1, 0).astype(bf16)
        r = dot(y1, t1[s], 1, 0) + dot(g, e, 1, 0)
        o_ref[:, xb * BG:xb * BG + 256] = (r[:, :256] + dot(y0, t0[s], 1, 0)).astype(bf16)
        o_ref[:, xb * BG + 256:xb * BG + TOP] = r[:, 256:].astype(bf16)
        o_ref[:, xb * BG + TOP:(xb + 1) * BG] = g


def apply(at, left, own, part, two):
    any_space = pl.BlockSpec(memory_space=pl.ANY)
    return pl.pallas_call(
        apply_kernel,
        out_shape=jax.ShapeDtypeStruct((BA, 16 * BG), bf16),
        grid_spec=pltpu.PrefetchScalarGridSpec(
            num_scalar_prefetch=1,
            grid=(4,),
            in_specs=[pl.BlockSpec((1, 4, BA, BG), lambda d, s: (d, 0, 0, 0))]
            + [any_space] * 8
            + [pl.BlockSpec((4, LAST, NB), lambda d, s: (0, 0, 0))] * 4,
            out_specs=pl.BlockSpec((BA, 4 * BG), lambda d, s: (0, lax.rem(s[1] - d + 4, 4))),
            scratch_shapes=[
                pltpu.VMEM((2, 4, PACK // 2, TOP), bf16),
                pltpu.VMEM((2, 4, PACK // 2, TOP), bf16),
                pltpu.VMEM((4, 4, LAST, NB), bf16),
                pltpu.VMEM((2, 256, 256), bf16),
                pltpu.VMEM((2, 256, TOP), bf16),
                pltpu.VMEM((2, REST, AP), bf16),
                pltpu.SemaphoreType.DMA((2,)),
                pltpu.SemaphoreType.DMA((2, 4)),
            ],
        ),
        compiler_params=VMEM,
        cost_estimate=cost(25),
    )(at, left, *own, *part, *two)


def tie(*arrays):
    return lax.optimization_barrier(arrays)


def shards(layer_inputs, output_grads, weight_grad):
    x, y, zh, zl, c = (lax.axis_index(n) for n in ("x", "y", "zh", "zl", "c"))
    zc = jnp.stack([2 * zh + zl, c]).astype(jnp.int32)
    at = jnp.stack([x, y, zh, c]).astype(jnp.int32)

    t = turn(output_grads, BG, lambda b: 4 * (b % 4) + b // 4, 5)
    t, weight_grad, layer_inputs = tie(t, weight_grad, layer_inputs)
    t = lax.all_to_all(t, ("x", "y"), 0, 0, tiled=True)
    w = weight_grad.reshape(BA, 2, BG).transpose(1, 0, 2)
    w_far = swap_zh(w)
    u = turn(layer_inputs, BA, lambda b: b, 2)
    w = jnp.concatenate([w, w_far], axis=0)
    t, w, u = tie(t, w, u)
    w1, w3 = along_y(w, 1), along_y(w, 3)
    mine, other = gram(zc, t)
    own, part = sum_over_copies(mine, other)
    m, t1 = first_inverse(zc, own, part)
    m, t1, w1, w3, u = tie(m, t1, w1, w3, u)
    w2 = [along_y(w1[:2], 1), along_y(w3[2:], 3)]
    q1 = near(t1)
    u = lax.all_to_all(u, ("x", "y"), 0, 0, tiled=True)
    a = small_gram(u)
    m, q1, a, *w2 = tie(m, q1, a, *w2)
    one = far(q1)
    q1_other = swap_core(q1)
    t2 = second_inverse(m)
    t2, a, q1_other, one[1], one[3] = tie(t2, a, q1_other, one[1], one[3])
    q2 = near(t2)
    a = small_sum(a, c)
    q2, a = tie(q2, a)
    two = far(q2)
    act = small_inverse(a)
    act, one[2], *two = tie(act, one[2], *two)
    act = move(act, ("zl", "c", "y"), lambda zl, c, y: (y >> 1, y & 1, 2 * zl + c))
    left = left_rows(at, act, [w, w1, *w2, w3])
    one_other = [q1_other] + [swap_core(v) for v in one[1:]]
    return apply(at, left, one, one_other, two)


def solution(mesh):
    fine = Mesh(np.asarray(mesh.devices).reshape(tuple(SIZES.values())), tuple(SIZES))
    dp, owner = ("x", "zl", "c"), ("y", "zh")
    return jax.shard_map(
        shards,
        mesh=fine,
        in_specs=(P(dp + owner, None), P(dp + owner, None), P(dp, owner)),
        out_specs=P(dp, None),
        check_vma=False,
    )
```

```python
import functools
import jax, jax.numpy as jnp
from jax import lax
from jax.experimental import pallas as pl
from jax.experimental.pallas import tpu as pltpu
f32=jnp.float32; bf16=jnp.bfloat16
NB=128

def split3(x):
    h=x.astype(bf16); r=x-h.astype(f32)
    m=r.astype(bf16); l=(r-m.astype(f32)).astype(bf16)
    return h,m,l

def bc(x,j):
    return jnp.broadcast_to(x[j:j+1,:],(8,128))

def tree(v):
    while len(v)>1:
        v=[a+b for a,b in zip(v[::2],v[1::2])]+([v[-1]] if len(v)%2 else [])
    return v[0]

def eliminate(chains):
    lane=lax.broadcasted_iota(jnp.int32,(8,128),1); sub=lax.broadcasted_iota(jnp.int32,(8,128),0)
    outs=[[] for _ in chains]
    for g in range(16):
        lo=8*g
        ing=(lane>=lo)&(lane<lo+8)
        eye=jnp.where(lane-lo==sub,1.0,0.0).astype(f32)
        st=[]
        for rows in chains:
            R=rows[g]
            B=[jnp.broadcast_to(R[:,lo+j:lo+j+1],(8,128)) for j in range(8)]
            S={(i,q):bc(B[q],i) for q in range(8) for i in range(q+1)}
            st.append([jnp.where(ing,eye,R),B,jnp.zeros((8,128),f32),S])
        for j in range(8):
            for s_ in st:
                R,B,U,S=s_
                p=S[j,j]
                r0=pl.reciprocal(p,approx=True)
                e=2.0-p*r0
                inv=r0*e
                for i in range(j+1,8):
                    for q in range(i,8):
                        S[i,q]=S[i,q]-((S[j,i]*S[j,q])*r0)*e
                rs=lax.rsqrt(p)
                rs=rs*(1.5-0.5*p*rs*rs)
                b=bc(R,j)
                U=jnp.where(sub==j,b*rs,U)
                m=b*inv
                R=jnp.where(sub==j,m,R-B[j]*m)
                for q in range(j+1,8):
                    s=S[j,q]*inv
                    B[q]=jnp.where(sub==j,s,B[q]-B[j]*s)
                s_[0]=R; s_[2]=U
        for ci,(rows,s_) in enumerate(zip(chains,st)):
            W=s_[0]; outs[ci].append(s_[2])
            w=[bc(W,j) for j in range(8)]
            for i in range(g+1,16):
                a=rows[i]
                rows[i]=jnp.where(ing,0.0,a)-tree([jnp.broadcast_to(a[:,lo+j:lo+j+1],(8,128))*w[j] for j in range(8)])
    return outs

def dot(a,b,ca,cb):
    return lax.dot_general(a,b,(((ca,),(cb,)),((),())),preferred_element_type=f32)

def load_diag(M,k,off=0):
    cols=pl.ds(pl.multiple_of(k*NB,NB),NB)
    return [M[pl.ds(pl.multiple_of((k-off)*NB+8*i,8),8),cols] for i in range(16)]

def store_lower(LD,rows):
    lane=lax.broadcasted_iota(jnp.int32,(8,128),1); sub=lax.broadcasted_iota(jnp.int32,(8,128),0)
    for i,u in enumerate(rows):
        LD[8*i:8*i+8,:]=jnp.where(lane<=sub+8*i,u,0.0)

def eye(n):
    return jnp.where(lax.broadcasted_iota(jnp.int32,(n,n),0)==lax.broadcasted_iota(jnp.int32,(n,n),1),1.0,0.0).astype(f32)

def panel(M,LD,k,n,off=0):
    nb=n//NB; c0=k*NB; r0=c0-off*NB
    M[r0:r0+NB,c0:c0+NB]=eye(NB)
    lh,lm,ll=split3(LD[...])
    mh,mm,ml=split3(M[r0:r0+NB,:])
    hm=jnp.concatenate([mh,mm],0); lhh=jnp.concatenate([ml,mh],0)
    U=dot(jnp.concatenate([lh,lh],1),hm,1,0)+dot(jnp.concatenate([lm,lm],1),hm,1,0)+dot(jnp.concatenate([lh,ll],1),lhh,1,0)
    M[r0:r0+NB,:]=U
    if k+1<nb:
        h,m,l=split3(U)
        c,r=c0+NB,r0+NB
        hm=jnp.concatenate([h,m],0); lhh=jnp.concatenate([l,h],0)
        ht,mt,lt=h[:,c:].T,m[:,c:].T,l[:,c:].T
        S=dot(jnp.concatenate([ht,ht],1),hm,1,0)+dot(jnp.concatenate([mt,mt],1),hm,1,0)+dot(jnp.concatenate([ht,lt],1),lhh,1,0)
        M[r:,c0:c]=jnp.zeros((n-c,NB),f32)
        M[r:,:]=M[r:,:]-S

def each(k,ks,f):
    for kk in ks:
        @pl.when(k==kk)
        def _(): f(kk)

def steps(M,LD,n,ks,off=0,Ma=None,LDa=None,na=0):
    def body(k,_):
        blocks=[load_diag(M,k,off)]
        if Ma is not None: blocks.append(load_diag(Ma,k-ks[0]))
        out=eliminate(blocks)
        store_lower(LD,out[0])
        if Ma is not None: store_lower(LDa,out[1])
        def both(kk):
            panel(M,LD,kk,n,off)
            if Ma is not None: panel(Ma,LDa,kk-ks[0],na)
        each(k,ks,both)
        return 0
    lax.fori_loop(ks[0],ks[-1]+1,body,0)


import itertools
import math
import numpy as np
from jax.sharding import Mesh, PartitionSpec as P

BA = 320
BG = 864
GP = 896
AP = 384
TOKENS = 16384.0
DAMPING = 0.1
SIZES = dict(x=4, zl=2, c=2, y=4, zh=2)
GB = [(i, j) for i in range(GP // NB) for j in range(i, GP // NB)]
AB = [(i, j) for i in range(AP // NB) for j in range(i, AP // NB)]
ROWS = len(GB) * NB
CHUNK = ROWS // 8
VMEM = pltpu.CompilerParams(vmem_limit_bytes=56 << 20)


def move(a, names, target):
    dims = [SIZES[n] for n in names]
    pairs = []
    for at in itertools.product(*map(range, dims)):
        to = target(*at)
        pairs.append((int(np.ravel_multi_index(at, dims)), int(np.ravel_multi_index(to, dims))))
    return lax.ppermute(a, names, pairs)


def along_z(a, d):
    def target(zl, zh):
        z = (2 * zh + zl + d) % 4
        return z % 2, z // 2
    return move(a, ("zl", "zh"), target)


def along_y(a, d):
    return move(a, ("y",), lambda y: ((y + d) % 4,))


def swap_core(a):
    return move(a, ("c",), lambda c: (1 - c,))


def swap_zh(a):
    return move(a, ("zh",), lambda h: (1 - h,))


def in_plane(a, d, first):
    def target(x, c, y):
        return ((x + d) % 4, c, y) if (c == 0) == first else (x, c, (y + d) % 4)
    return move(a, ("x", "c", "y"), target)


def cost(us):
    return pl.CostEstimate(flops=int(us * 1e9), bytes_accessed=1 << 20, transcendentals=0)


def turn_kernel(size, slot, g_ref, o_ref):
    for t in range(g_ref.shape[1] // NB):
        tile = g_ref[:, t * NB:(t + 1) * NB].T
        at, end = t * NB, (t + 1) * NB
        while at < end:
            b = at // size
            stop = min(end, (b + 1) * size)
            o_ref[slot(b), at - b * size:stop - b * size, :] = tile[at - t * NB:stop - t * NB, :]
            at = stop


def turn(g, size, slot, us):
    return pl.pallas_call(
        functools.partial(turn_kernel, size, slot),
        out_shape=jax.ShapeDtypeStruct((16, size, NB), bf16),
        compiler_params=VMEM,
        cost_estimate=cost(us),
    )(g)


def products(t_ref, s_ref, p_ref, size, n, blocks):
    if size < n:
        s_ref[size:, :] = jnp.zeros((n - size, 16 * NB), bf16)
    for s in range(16):
        s_ref[:size, s * NB:(s + 1) * NB] = t_ref[s]
    for r0 in range(0, n, 2 * NB):
        rows = min(2 * NB, n - r0)
        d = dot(s_ref[r0:r0 + rows, :], s_ref[r0:, :], 1, 1)
        for k, (i, j) in enumerate(blocks):
            if r0 <= i * NB < r0 + rows:
                p_ref[k * NB:(k + 1) * NB, :] = d[i * NB - r0:(i + 1) * NB - r0, j * NB - r0:(j + 1) * NB - r0]


def gram_kernel(at_ref, t_ref, mine_ref, other_ref, s_ref, p_ref):
    z, c = at_ref[0], at_ref[1]
    products(t_ref, s_ref, p_ref, BG, GP, GB)
    for q in range(4):
        d = lax.rem(q - z + 4, 4)
        rows = pl.ds(pl.multiple_of(d * CHUNK, 8), CHUNK)
        first, second = p_ref[q * CHUNK:(q + 1) * CHUNK, :], p_ref[(4 + q) * CHUNK:(5 + q) * CHUNK, :]
        mine_ref[rows, :] = jnp.where(c == 0, first, second)
        other_ref[rows, :] = jnp.where(c == 0, second, first)


def gram(at, t):
    half = jax.ShapeDtypeStruct((4 * CHUNK, NB), f32)
    return pl.pallas_call(
        gram_kernel,
        out_shape=(half, half),
        in_specs=[pl.BlockSpec(memory_space=pltpu.SMEM), pl.BlockSpec(memory_space=pltpu.VMEM)],
        scratch_shapes=[pltpu.VMEM((GP, 16 * NB), bf16), pltpu.VMEM((ROWS, NB), f32)],
        compiler_params=VMEM,
        cost_estimate=cost(8),
    )(at, t)


def small_gram_kernel(t_ref, p_ref, s_ref):
    products(t_ref, s_ref, p_ref, BA, AP, AB)


def small_gram(t):
    return pl.pallas_call(
        small_gram_kernel,
        out_shape=jax.ShapeDtypeStruct((len(AB) * NB, NB), f32),
        scratch_shapes=[pltpu.VMEM((AP, 16 * NB), bf16)],
        compiler_params=VMEM,
        cost_estimate=cost(3),
    )(t)


def sum_over_copies(mine, other):
    h = mine + swap_core(other)
    part = [h[d * CHUNK:(d + 1) * CHUNK] for d in range(4)]
    got = [along_z(part[d], d) for d in (1, 2, 3)]
    s = part[0] + got[0] + got[1] + got[2]
    own = jnp.concatenate([s] + [along_z(s, d) for d in (1, 2, 3)], axis=0)
    return own, swap_core(own)


def small_sum(p, c):
    half = len(AB) * NB // 2
    first, second = p[:half], p[half:]
    h = jnp.where(c == 0, first, second) + swap_core(jnp.where(c == 0, second, first))
    got = [along_z(h, d) for d in (1, 2, 3)]
    s = (h + got[1]) + (got[0] + got[2])
    o = swap_core(s)
    return jnp.concatenate([jnp.where(c == 0, s, o), jnp.where(c == 0, o, s)], axis=0)


def unpack(M, n, blocks, p_ref):
    M[...] = jnp.zeros((n, n), f32)
    for k, (i, j) in enumerate(blocks):
        block = p_ref[k * NB:(k + 1) * NB, :] / TOKENS
        if i == j:
            block = block + DAMPING * eye(NB)
        M[i * NB:(i + 1) * NB, j * NB:(j + 1) * NB] = block


def lower():
    return lax.broadcasted_iota(jnp.int32, (NB, NB), 0) >= lax.broadcasted_iota(jnp.int32, (NB, NB), 1)


TOP = 512
REST = BG - TOP
PACK = 128 + 256 + REST


def tidy(M, n):
    for i in range(n // NB):
        M[i * NB:(i + 1) * NB, i * NB:(i + 1) * NB] = jnp.where(lower(), M[i * NB:(i + 1) * NB, i * NB:(i + 1) * NB], 0.0)


def first_kernel(at_ref, own_ref, part_ref, m_ref, t_ref, p_ref, M, LD, s_ref):
    z, c = at_ref[0], at_ref[1]
    for d in range(4):
        q = lax.rem(z - d + 4, 4)
        p_ref[pl.ds(pl.multiple_of((4 * c + q) * CHUNK, 8), CHUNK), :] = own_ref[d * CHUNK:(d + 1) * CHUNK, :]
        p_ref[pl.ds(pl.multiple_of((4 * (1 - c) + q) * CHUNK, 8), CHUNK), :] = part_ref[d * CHUNK:(d + 1) * CHUNK, :]
    unpack(M, GP, GB, p_ref)
    steps(M, LD, GP, range(4))
    m_ref[...] = M[TOP:, TOP:]
    tidy(M, TOP)
    for i in (0, 2):
        M[i * NB:(i + 1) * NB, (i + 1) * NB:(i + 2) * NB] = jnp.zeros((NB, NB), f32)
    s_ref[0:128, 0:256] = M[0:128, 0:256].astype(bf16)
    s_ref[0:128, 256:512] = M[128:256, 0:256].astype(bf16)
    s_ref[128:384, :] = M[256:512, :TOP].astype(bf16)
    s_ref[384:, :] = M[TOP:BG, :TOP].astype(bf16)
    t_ref[...] = s_ref[pl.ds(pl.multiple_of(c * (PACK // 2), 16), PACK // 2), :]


def first_inverse(at, own, part):
    return pl.pallas_call(
        first_kernel,
        out_shape=(jax.ShapeDtypeStruct((AP, AP), f32), jax.ShapeDtypeStruct((PACK // 2, TOP), bf16)),
        in_specs=[pl.BlockSpec(memory_space=pltpu.SMEM)] + [pl.BlockSpec(memory_space=pltpu.VMEM)] * 2,
        scratch_shapes=[
            pltpu.VMEM((ROWS, NB), f32),
            pltpu.VMEM((GP, GP), f32),
            pltpu.VMEM((NB, NB), f32),
            pltpu.VMEM((PACK, TOP), bf16),
        ],
        compiler_params=VMEM,
        cost_estimate=cost(2),
    )(at, own, part)


def second_kernel(m_in, t_ref, M, LD):
    M[...] = m_in[...]
    steps(M, LD, AP, range(3))
    tidy(M, AP)
    at = 0
    for i in range(3):
        rows = min(NB, REST - i * NB)
        for j in range(i + 1):
            t_ref[at:at + rows, :] = M[i * NB:i * NB + rows, j * NB:(j + 1) * NB].astype(bf16)
            at += rows


LAST = 3 * NB + 3 * (REST - 2 * NB)


def second_inverse(m):
    return pl.pallas_call(
        second_kernel,
        out_shape=jax.ShapeDtypeStruct((LAST, NB), bf16),
        scratch_shapes=[pltpu.VMEM((AP, AP), f32), pltpu.VMEM((NB, NB), f32)],
        compiler_params=VMEM,
        cost_estimate=cost(1),
    )(m)


def small_inverse_kernel(a_in, inv_ref, M, LD):
    unpack(M, AP, AB, a_in)
    steps(M, LD, AP, range(3))
    tidy(M, AP)
    n = AP // NB
    for i in range(n):
        for j in range(i + 1, n):
            M[i * NB:(i + 1) * NB, j * NB:(j + 1) * NB] = jnp.zeros((NB, NB), f32)
    L = M[:BA, :BA]
    inv_ref[...] = lax.dot_general(
        L, L, (((0,), (0,)), ((), ())), precision=lax.Precision.HIGHEST, preferred_element_type=f32
    ).astype(bf16)


def small_inverse(a):
    return pl.pallas_call(
        small_inverse_kernel,
        out_shape=jax.ShapeDtypeStruct((BA, BA), bf16),
        scratch_shapes=[pltpu.VMEM((AP, AP), f32), pltpu.VMEM((NB, NB), f32)],
        compiler_params=VMEM,
        cost_estimate=cost(1),
    )(a)


def near(t):
    return jnp.stack([t] + [in_plane(t, d, True) for d in (1, 2, 3)])


def far(q):
    return [q] + [in_plane(q, d, False) for d in (1, 2, 3)]


def left_kernel(at_ref, act_ref, *refs):
    w, (o_ref, wv, sem) = refs[0:5], refs[5:]
    d, zh = pl.program_id(0), at_ref[2]

    def copies(k):
        if k == 2:
            return [
                pltpu.make_async_copy(w[2], wv.at[2, 0:2], sem.at[2]),
                pltpu.make_async_copy(w[3], wv.at[2, 2:4], sem.at[4]),
            ]
        return [pltpu.make_async_copy(w[(0, 1, None, 4)[k]], wv.at[k], sem.at[k])]

    @pl.when(d == 0)
    def _():
        for k in range(4):
            for m in copies(k):
                m.start()

    for k in range(4):
        @pl.when(d == k)
        def _():
            for m in copies(k):
                m.wait()
    for xb in range(4):
        zb, h = xb // 2, xb % 2
        o_ref[0, xb] = dot(act_ref[...], wv[d, 2 * jnp.where(zh == zb, 0, 1) + h], 1, 0).astype(bf16)


def left_rows(at, act, w):
    return pl.pallas_call(
        left_kernel,
        out_shape=jax.ShapeDtypeStruct((4, 4, BA, BG), bf16),
        grid_spec=pltpu.PrefetchScalarGridSpec(
            num_scalar_prefetch=1,
            grid=(4,),
            in_specs=[pl.BlockSpec((BA, BA), lambda d, s: (0, 0))] + [pl.BlockSpec(memory_space=pl.ANY)] * 5,
            out_specs=pl.BlockSpec((1, 4, BA, BG), lambda d, s: (d, 0, 0, 0)),
            scratch_shapes=[pltpu.VMEM((4, 4, BA, BG), bf16), pltpu.SemaphoreType.DMA((5,))],
        ),
        compiler_params=VMEM,
        cost_estimate=cost(8),
    )(at, act, *w)


def apply_kernel(at_ref, l_ref, *refs):
    own, part, two = refs[0:4], refs[4:8], refs[8:12]
    o_ref, va, vb, v, t0, t1, K, sema, semb = refs[12:]
    x, c = at_ref[0], at_ref[3]
    d = pl.program_id(0)
    slot = lax.rem(d, 2)

    def fetch(k):
        for core in range(2):
            @pl.when(c == core)
            def _():
                first, second = (own, part) if core == 0 else (part, own)
                pltpu.make_async_copy(first[k], va.at[k % 2], sema.at[k % 2]).start()
                for q in range(4):
                    pltpu.make_async_copy(second[q].at[k], vb.at[k % 2, q], semb.at[k % 2, q]).start()

    @pl.when(d == 0)
    def _():
        fetch(0)
        K[...] = jnp.zeros(K.shape, bf16)
        for k in range(4):
            v[k] = two[k][...]

    for k in range(3):
        @pl.when(d == k)
        def _():
            fetch(k + 1)

    pltpu.make_async_copy(own[0], va.at[slot], sema.at[slot]).wait()
    for q in range(4):
        pltpu.make_async_copy(own[0].at[0], vb.at[slot, q], semb.at[slot, q]).wait()

    half = PACK // 2
    for xb in range(4):
        dx = lax.rem(x - xb + 4, 4)
        s = xb % 2
        t0[s, 0:128, :] = va[slot, dx, 0:128, 0:256]
        t0[s, 128:256, :] = va[slot, dx, 0:128, 256:512]
        t1[s, 0:half - 128, :] = va[slot, dx, 128:half, :]
        t1[s, half - 128:256, :] = vb[slot, dx, 0:384 - half, :]
        k = v.at[jnp.where(c == 0, d, dx), jnp.where(c == 0, dx, d)]
        at = 0
        for i in range(3):
            rows = min(NB, REST - i * NB)
            for j in range(i + 1):
                K[s, i * NB:i * NB + rows, j * NB:(j + 1) * NB] = k[at:at + rows, :]
                at += rows
        e = vb[slot, dx, 384 - half:half, :]
        kk = K[s][:, :REST]
        left = l_ref[0, xb]
        l0 = left[:, :TOP]
        u = (left[:, TOP:].astype(f32) + dot(l0, e, 1, 1)).astype(bf16)
        y0 = dot(l0[:, :256], t0[s], 1, 1).astype(bf16)
        y1 = dot(l0, t1[s], 1, 1).astype(bf16)
        g = dot(dot(u, kk, 1, 1).astype(bf16), kk, 1, 0).astype(bf16)
        r = dot(y1, t1[s], 1, 0) + dot(g, e, 1, 0)
        o_ref[:, xb * BG:xb * BG + 256] = (r[:, :256] + dot(y0, t0[s], 1, 0)).astype(bf16)
        o_ref[:, xb * BG + 256:xb * BG + TOP] = r[:, 256:].astype(bf16)
        o_ref[:, xb * BG + TOP:(xb + 1) * BG] = g


def apply(at, left, own, part, two):
    any_space = pl.BlockSpec(memory_space=pl.ANY)
    return pl.pallas_call(
        apply_kernel,
        out_shape=jax.ShapeDtypeStruct((BA, 16 * BG), bf16),
        grid_spec=pltpu.PrefetchScalarGridSpec(
            num_scalar_prefetch=1,
            grid=(4,),
            in_specs=[pl.BlockSpec((1, 4, BA, BG), lambda d, s: (d, 0, 0, 0))]
            + [any_space] * 8
            + [pl.BlockSpec((4, LAST, NB), lambda d, s: (0, 0, 0))] * 4,
            out_specs=pl.BlockSpec((BA, 4 * BG), lambda d, s: (0, lax.rem(s[1] - d + 4, 4))),
            scratch_shapes=[
                pltpu.VMEM((2, 4, PACK // 2, TOP), bf16),
                pltpu.VMEM((2, 4, PACK // 2, TOP), bf16),
                pltpu.VMEM((4, 4, LAST, NB), bf16),
                pltpu.VMEM((2, 256, 256), bf16),
                pltpu.VMEM((2, 256, TOP), bf16),
                pltpu.VMEM((2, REST, AP), bf16),
                pltpu.SemaphoreType.DMA((2,)),
                pltpu.SemaphoreType.DMA((2, 4)),
            ],
        ),
        compiler_params=VMEM,
        cost_estimate=cost(25),
    )(at, left, *own, *part, *two)


def tie(*arrays):
    return lax.optimization_barrier(arrays)


def shards(layer_inputs, output_grads, weight_grad):
    x, y, zh, zl, c = (lax.axis_index(n) for n in ("x", "y", "zh", "zl", "c"))
    zc = jnp.stack([2 * zh + zl, c]).astype(jnp.int32)
    at = jnp.stack([x, y, zh, c]).astype(jnp.int32)

    t = turn(output_grads, BG, lambda b: 4 * (b % 4) + b // 4, 5)
    t, weight_grad, layer_inputs = tie(t, weight_grad, layer_inputs)
    t = lax.all_to_all(t, ("x", "y"), 0, 0, tiled=True)
    w = weight_grad.reshape(BA, 2, BG).transpose(1, 0, 2)
    w_far = swap_zh(w)
    u = turn(layer_inputs, BA, lambda b: b, 2)
    w = jnp.concatenate([w, w_far], axis=0)
    t, w, u = tie(t, w, u)
    w1, w3 = along_y(w, 1), along_y(w, 3)
    mine, other = gram(zc, t)
    mine, other, u = tie(mine, other, u)
    u = lax.all_to_all(u, ("x", "y"), 0, 0, tiled=True)
    own, part = sum_over_copies(mine, other)
    m, t1 = first_inverse(zc, own, part)
    m, t1, w1, w3, u = tie(m, t1, w1, w3, u)
    w2 = [along_y(w1[:2], 1), along_y(w3[2:], 3)]
    q1 = near(t1)
    a = small_gram(u)
    m, q1, a = tie(m, q1, a)
    one = far(q1)
    q1_other = swap_core(q1)
    t2 = second_inverse(m)
    t2, a, q1_other, one[1], one[3] = tie(t2, a, q1_other, one[1], one[3])
    q2 = near(t2)
    a = small_sum(a, c)
    q2, a, *w2 = tie(q2, a, *w2)
    two = far(q2)
    act = small_inverse(a)
    act, one[2], *two = tie(act, one[2], *two)
    act = move(act, ("zl", "c", "y"), lambda zl, c, y: (y >> 1, y & 1, 2 * zl + c))
    left = left_rows(at, act, [w, w1, *w2, w3])
    one_other = [q1_other] + [swap_core(v) for v in one[1:]]
    return apply(at, left, one, one_other, two)


def solution(mesh):
    fine = Mesh(np.asarray(mesh.devices).reshape(tuple(SIZES.values())), tuple(SIZES))
    dp, owner = ("x", "zl", "c"), ("y", "zh")
    return jax.shard_map(
        shards,
        mesh=fine,
        in_specs=(P(dp + owner, None), P(dp + owner, None), P(dp, owner)),
        out_specs=P(dp, None),
        check_vma=False,
    )
```

```python
import functools
import jax, jax.numpy as jnp
from jax import lax
from jax.experimental import pallas as pl
from jax.experimental.pallas import tpu as pltpu
f32=jnp.float32; bf16=jnp.bfloat16
NB=128

def split3(x):
    h=x.astype(bf16); r=x-h.astype(f32)
    m=r.astype(bf16); l=(r-m.astype(f32)).astype(bf16)
    return h,m,l

def bc(x,j):
    return jnp.broadcast_to(x[j:j+1,:],(8,128))

def tree(v):
    while len(v)>1:
        v=[a+b for a,b in zip(v[::2],v[1::2])]+([v[-1]] if len(v)%2 else [])
    return v[0]

def eliminate(chains):
    lane=lax.broadcasted_iota(jnp.int32,(8,128),1); sub=lax.broadcasted_iota(jnp.int32,(8,128),0)
    outs=[[] for _ in chains]
    for g in range(16):
        lo=8*g
        ing=(lane>=lo)&(lane<lo+8)
        eye=jnp.where(lane-lo==sub,1.0,0.0).astype(f32)
        st=[]
        for rows in chains:
            R=rows[g]
            B=[jnp.broadcast_to(R[:,lo+j:lo+j+1],(8,128)) for j in range(8)]
            S={(i,q):bc(B[q],i) for q in range(8) for i in range(q+1)}
            st.append([jnp.where(ing,eye,R),B,jnp.zeros((8,128),f32),S])
        for j in range(8):
            for s_ in st:
                R,B,U,S=s_
                p=S[j,j]
                r0=pl.reciprocal(p,approx=True)
                e=2.0-p*r0
                inv=r0*e
                for i in range(j+1,8):
                    for q in range(i,8):
                        S[i,q]=S[i,q]-((S[j,i]*S[j,q])*r0)*e
                rs=lax.rsqrt(p)
                rs=rs*(1.5-0.5*p*rs*rs)
                b=bc(R,j)
                U=jnp.where(sub==j,b*rs,U)
                m=b*inv
                R=jnp.where(sub==j,m,R-B[j]*m)
                for q in range(j+1,8):
                    s=S[j,q]*inv
                    B[q]=jnp.where(sub==j,s,B[q]-B[j]*s)
                s_[0]=R; s_[2]=U
        for ci,(rows,s_) in enumerate(zip(chains,st)):
            W=s_[0]; outs[ci].append(s_[2])
            w=[bc(W,j) for j in range(8)]
            for i in range(g+1,16):
                a=rows[i]
                rows[i]=jnp.where(ing,0.0,a)-tree([jnp.broadcast_to(a[:,lo+j:lo+j+1],(8,128))*w[j] for j in range(8)])
    return outs

def dot(a,b,ca,cb):
    return lax.dot_general(a,b,(((ca,),(cb,)),((),())),preferred_element_type=f32)

def load_diag(M,k,off=0):
    cols=pl.ds(pl.multiple_of(k*NB,NB),NB)
    return [M[pl.ds(pl.multiple_of((k-off)*NB+8*i,8),8),cols] for i in range(16)]

def store_lower(LD,rows):
    lane=lax.broadcasted_iota(jnp.int32,(8,128),1); sub=lax.broadcasted_iota(jnp.int32,(8,128),0)
    for i,u in enumerate(rows):
        LD[8*i:8*i+8,:]=jnp.where(lane<=sub+8*i,u,0.0)

def eye(n):
    return jnp.where(lax.broadcasted_iota(jnp.int32,(n,n),0)==lax.broadcasted_iota(jnp.int32,(n,n),1),1.0,0.0).astype(f32)

def panel(M,LD,k,n,off=0):
    nb=n//NB; c0=k*NB; r0=c0-off*NB
    M[r0:r0+NB,c0:c0+NB]=eye(NB)
    lh,lm,ll=split3(LD[...])
    mh,mm,ml=split3(M[r0:r0+NB,:])
    hm=jnp.concatenate([mh,mm],0); lhh=jnp.concatenate([ml,mh],0)
    U=dot(jnp.concatenate([lh,lh],1),hm,1,0)+dot(jnp.concatenate([lm,lm],1),hm,1,0)+dot(jnp.concatenate([lh,ll],1),lhh,1,0)
    M[r0:r0+NB,:]=U
    if k+1<nb:
        h,m,l=split3(U)
        c,r=c0+NB,r0+NB
        hm=jnp.concatenate([h,m],0); lhh=jnp.concatenate([l,h],0)
        ht,mt,lt=h[:,c:].T,m[:,c:].T,l[:,c:].T
        S=dot(jnp.concatenate([ht,ht],1),hm,1,0)+dot(jnp.concatenate([mt,mt],1),hm,1,0)+dot(jnp.concatenate([ht,lt],1),lhh,1,0)
        M[r:,c0:c]=jnp.zeros((n-c,NB),f32)
        M[r:,:]=M[r:,:]-S

def each(k,ks,f):
    for kk in ks:
        @pl.when(k==kk)
        def _(): f(kk)

def steps(M,LD,n,ks,off=0,Ma=None,LDa=None,na=0):
    def body(k,_):
        blocks=[load_diag(M,k,off)]
        if Ma is not None: blocks.append(load_diag(Ma,k-ks[0]))
        out=eliminate(blocks)
        store_lower(LD,out[0])
        if Ma is not None: store_lower(LDa,out[1])
        def both(kk):
            panel(M,LD,kk,n,off)
            if Ma is not None: panel(Ma,LDa,kk-ks[0],na)
        each(k,ks,both)
        return 0
    lax.fori_loop(ks[0],ks[-1]+1,body,0)


import itertools
import math
import numpy as np
from jax.sharding import Mesh, PartitionSpec as P

BA = 320
BG = 864
GP = 896
AP = 384
TOKENS = 16384.0
DAMPING = 0.1
SIZES = dict(x=4, zl=2, c=2, y=4, zh=2)
GB = [(i, j) for i in range(GP // NB) for j in range(i, GP // NB)]
AB = [(i, j) for i in range(AP // NB) for j in range(i, AP // NB)]
ROWS = len(GB) * NB
CHUNK = ROWS // 8
VMEM = pltpu.CompilerParams(vmem_limit_bytes=56 << 20)


def move(a, names, target):
    dims = [SIZES[n] for n in names]
    pairs = []
    for at in itertools.product(*map(range, dims)):
        to = target(*at)
        pairs.append((int(np.ravel_multi_index(at, dims)), int(np.ravel_multi_index(to, dims))))
    return lax.ppermute(a, names, pairs)


def along_z(a, d):
    def target(zl, zh):
        z = (2 * zh + zl + d) % 4
        return z % 2, z // 2
    return move(a, ("zl", "zh"), target)


def along_y(a, d):
    return move(a, ("y",), lambda y: ((y + d) % 4,))


def swap_core(a):
    return move(a, ("c",), lambda c: (1 - c,))


def swap_zh(a):
    return move(a, ("zh",), lambda h: (1 - h,))


def in_plane(a, d, first):
    def target(x, c, y):
        return ((x + d) % 4, c, y) if (c == 0) == first else (x, c, (y + d) % 4)
    return move(a, ("x", "c", "y"), target)


def cost(us):
    return pl.CostEstimate(flops=int(us * 1e9), bytes_accessed=1 << 20, transcendentals=0)


def turn_kernel(size, slot, g_ref, o_ref):
    for t in range(g_ref.shape[1] // NB):
        tile = g_ref[:, t * NB:(t + 1) * NB].T
        at, end = t * NB, (t + 1) * NB
        while at < end:
            b = at // size
            stop = min(end, (b + 1) * size)
            o_ref[slot(b), at - b * size:stop - b * size, :] = tile[at - t * NB:stop - t * NB, :]
            at = stop


def turn(g, size, slot, us):
    return pl.pallas_call(
        functools.partial(turn_kernel, size, slot),
        out_shape=jax.ShapeDtypeStruct((16, size, NB), bf16),
        compiler_params=VMEM,
        cost_estimate=cost(us),
    )(g)


def products(t_ref, s_ref, p_ref, size, n, blocks):
    if size < n:
        s_ref[size:, :] = jnp.zeros((n - size, 16 * NB), bf16)
    for s in range(16):
        s_ref[:size, s * NB:(s + 1) * NB] = t_ref[s]
    for r0 in range(0, n, 2 * NB):
        rows = min(2 * NB, n - r0)
        d = dot(s_ref[r0:r0 + rows, :], s_ref[r0:, :], 1, 1)
        for k, (i, j) in enumerate(blocks):
            if r0 <= i * NB < r0 + rows:
                p_ref[k * NB:(k + 1) * NB, :] = d[i * NB - r0:(i + 1) * NB - r0, j * NB - r0:(j + 1) * NB - r0]


def gram_kernel(at_ref, t_ref, mine_ref, other_ref, s_ref, p_ref):
    z, c = at_ref[0], at_ref[1]
    products(t_ref, s_ref, p_ref, BG, GP, GB)
    for q in range(4):
        d = lax.rem(q - z + 4, 4)
        rows = pl.ds(pl.multiple_of(d * CHUNK, 8), CHUNK)
        first, second = p_ref[q * CHUNK:(q + 1) * CHUNK, :], p_ref[(4 + q) * CHUNK:(5 + q) * CHUNK, :]
        mine_ref[rows, :] = jnp.where(c == 0, first, second)
        other_ref[rows, :] = jnp.where(c == 0, second, first)


def gram(at, t):
    half = jax.ShapeDtypeStruct((4 * CHUNK, NB), f32)
    return pl.pallas_call(
        gram_kernel,
        out_shape=(half, half),
        in_specs=[pl.BlockSpec(memory_space=pltpu.SMEM), pl.BlockSpec(memory_space=pltpu.VMEM)],
        scratch_shapes=[pltpu.VMEM((GP, 16 * NB), bf16), pltpu.VMEM((ROWS, NB), f32)],
        compiler_params=VMEM,
        cost_estimate=cost(8),
    )(at, t)


def small_gram_kernel(t_ref, p_ref, s_ref):
    products(t_ref, s_ref, p_ref, BA, AP, AB)


def small_gram(t):
    return pl.pallas_call(
        small_gram_kernel,
        out_shape=jax.ShapeDtypeStruct((len(AB) * NB, NB), f32),
        scratch_shapes=[pltpu.VMEM((AP, 16 * NB), bf16)],
        compiler_params=VMEM,
        cost_estimate=cost(3),
    )(t)


def sum_over_copies(mine, other):
    h = mine + swap_core(other)
    part = [h[d * CHUNK:(d + 1) * CHUNK] for d in range(4)]
    got = [along_z(part[d], d) for d in (1, 2, 3)]
    s = part[0] + got[0] + got[1] + got[2]
    own = jnp.concatenate([s] + [along_z(s, d) for d in (1, 2, 3)], axis=0)
    return own, swap_core(own)


def small_sum(p, c):
    half = len(AB) * NB // 2
    first, second = p[:half], p[half:]
    h = jnp.where(c == 0, first, second) + swap_core(jnp.where(c == 0, second, first))
    got = [along_z(h, d) for d in (1, 2, 3)]
    s = (h + got[1]) + (got[0] + got[2])
    o = swap_core(s)
    return jnp.concatenate([jnp.where(c == 0, s, o), jnp.where(c == 0, o, s)], axis=0)


def unpack(M, n, blocks, p_ref):
    M[...] = jnp.zeros((n, n), f32)
    for k, (i, j) in enumerate(blocks):
        block = p_ref[k * NB:(k + 1) * NB, :] / TOKENS
        if i == j:
            block = block + DAMPING * eye(NB)
        M[i * NB:(i + 1) * NB, j * NB:(j + 1) * NB] = block


def lower():
    return lax.broadcasted_iota(jnp.int32, (NB, NB), 0) >= lax.broadcasted_iota(jnp.int32, (NB, NB), 1)


TOP = 512
REST = BG - TOP
PACK = 128 + 256 + REST


def tidy(M, n):
    for i in range(n // NB):
        M[i * NB:(i + 1) * NB, i * NB:(i + 1) * NB] = jnp.where(lower(), M[i * NB:(i + 1) * NB, i * NB:(i + 1) * NB], 0.0)


def first_kernel(at_ref, own_ref, part_ref, m_ref, t_ref, p_ref, M, LD, s_ref):
    z, c = at_ref[0], at_ref[1]
    for d in range(4):
        q = lax.rem(z - d + 4, 4)
        p_ref[pl.ds(pl.multiple_of((4 * c + q) * CHUNK, 8), CHUNK), :] = own_ref[d * CHUNK:(d + 1) * CHUNK, :]
        p_ref[pl.ds(pl.multiple_of((4 * (1 - c) + q) * CHUNK, 8), CHUNK), :] = part_ref[d * CHUNK:(d + 1) * CHUNK, :]
    unpack(M, GP, GB, p_ref)
    steps(M, LD, GP, range(4))
    m_ref[...] = M[TOP:, TOP:]
    tidy(M, TOP)
    for i in (0, 2):
        M[i * NB:(i + 1) * NB, (i + 1) * NB:(i + 2) * NB] = jnp.zeros((NB, NB), f32)
    s_ref[0:128, 0:256] = M[0:128, 0:256].astype(bf16)
    s_ref[0:128, 256:512] = M[128:256, 0:256].astype(bf16)
    s_ref[128:384, :] = M[256:512, :TOP].astype(bf16)
    s_ref[384:, :] = M[TOP:BG, :TOP].astype(bf16)
    t_ref[...] = s_ref[pl.ds(pl.multiple_of(c * (PACK // 2), 16), PACK // 2), :]


def first_inverse(at, own, part):
    return pl.pallas_call(
        first_kernel,
        out_shape=(jax.ShapeDtypeStruct((AP, AP), f32), jax.ShapeDtypeStruct((PACK // 2, TOP), bf16)),
        in_specs=[pl.BlockSpec(memory_space=pltpu.SMEM)] + [pl.BlockSpec(memory_space=pltpu.VMEM)] * 2,
        scratch_shapes=[
            pltpu.VMEM((ROWS, NB), f32),
            pltpu.VMEM((GP, GP), f32),
            pltpu.VMEM((NB, NB), f32),
            pltpu.VMEM((PACK, TOP), bf16),
        ],
        compiler_params=VMEM,
        cost_estimate=cost(2),
    )(at, own, part)


def second_kernel(m_in, t_ref, M, LD):
    M[...] = m_in[...]
    steps(M, LD, AP, range(3))
    tidy(M, AP)
    at = 0
    for i in range(3):
        rows = min(NB, REST - i * NB)
        for j in range(i + 1):
            t_ref[at:at + rows, :] = M[i * NB:i * NB + rows, j * NB:(j + 1) * NB].astype(bf16)
            at += rows


LAST = 3 * NB + 3 * (REST - 2 * NB)


def second_inverse(m):
    return pl.pallas_call(
        second_kernel,
        out_shape=jax.ShapeDtypeStruct((LAST, NB), bf16),
        scratch_shapes=[pltpu.VMEM((AP, AP), f32), pltpu.VMEM((NB, NB), f32)],
        compiler_params=VMEM,
        cost_estimate=cost(1),
    )(m)


def small_inverse_kernel(a_in, inv_ref, M, LD):
    unpack(M, AP, AB, a_in)
    steps(M, LD, AP, range(3))
    tidy(M, AP)
    n = AP // NB
    for i in range(n):
        for j in range(i + 1, n):
            M[i * NB:(i + 1) * NB, j * NB:(j + 1) * NB] = jnp.zeros((NB, NB), f32)
    L = M[:BA, :BA]
    inv_ref[...] = lax.dot_general(
        L, L, (((0,), (0,)), ((), ())), precision=lax.Precision.HIGHEST, preferred_element_type=f32
    ).astype(bf16)


def small_inverse(a):
    return pl.pallas_call(
        small_inverse_kernel,
        out_shape=jax.ShapeDtypeStruct((BA, BA), bf16),
        scratch_shapes=[pltpu.VMEM((AP, AP), f32), pltpu.VMEM((NB, NB), f32)],
        compiler_params=VMEM,
        cost_estimate=cost(1),
    )(a)


def near(t):
    return jnp.stack([t] + [in_plane(t, d, True) for d in (1, 2, 3)])


def far(q):
    return [q] + [in_plane(q, d, False) for d in (1, 2, 3)]


def left_kernel(at_ref, act_ref, *refs):
    w, (o_ref, wv, sem) = refs[0:5], refs[5:]
    d, zh = pl.program_id(0), at_ref[2]

    def copies(k):
        if k == 2:
            return [
                pltpu.make_async_copy(w[2], wv.at[2, 0:2], sem.at[2]),
                pltpu.make_async_copy(w[3], wv.at[2, 2:4], sem.at[4]),
            ]
        return [pltpu.make_async_copy(w[(0, 1, None, 4)[k]], wv.at[k], sem.at[k])]

    @pl.when(d == 0)
    def _():
        for k in range(4):
            for m in copies(k):
                m.start()

    for k in range(4):
        @pl.when(d == k)
        def _():
            for m in copies(k):
                m.wait()
    for xb in range(4):
        zb, h = xb // 2, xb % 2
        o_ref[0, xb] = dot(act_ref[...], wv[d, 2 * jnp.where(zh == zb, 0, 1) + h], 1, 0).astype(bf16)


def left_rows(at, act, w):
    return pl.pallas_call(
        left_kernel,
        out_shape=jax.ShapeDtypeStruct((4, 4, BA, BG), bf16),
        grid_spec=pltpu.PrefetchScalarGridSpec(
            num_scalar_prefetch=1,
            grid=(4,),
            in_specs=[pl.BlockSpec((BA, BA), lambda d, s: (0, 0))] + [pl.BlockSpec(memory_space=pl.ANY)] * 5,
            out_specs=pl.BlockSpec((1, 4, BA, BG), lambda d, s: (d, 0, 0, 0)),
            scratch_shapes=[pltpu.VMEM((4, 4, BA, BG), bf16), pltpu.SemaphoreType.DMA((5,))],
        ),
        compiler_params=VMEM,
        cost_estimate=cost(8),
    )(at, act, *w)


def apply_kernel(at_ref, l_ref, *refs):
    own, part, two = refs[0:4], refs[4:8], refs[8:12]
    o_ref, va, vb, v, t0, t1, K, sema, semb = refs[12:]
    x, c = at_ref[0], at_ref[3]
    d = pl.program_id(0)
    slot = lax.rem(d, 2)

    def fetch(k):
        for core in range(2):
            @pl.when(c == core)
            def _():
                first, second = (own, part) if core == 0 else (part, own)
                pltpu.make_async_copy(first[k], va.at[k % 2], sema.at[k % 2]).start()
                for q in range(4):
                    pltpu.make_async_copy(second[q].at[k], vb.at[k % 2, q], semb.at[k % 2, q]).start()

    @pl.when(d == 0)
    def _():
        fetch(0)
        K[...] = jnp.zeros(K.shape, bf16)
        for k in range(4):
            v[k] = two[k][...]

    for k in range(3):
        @pl.when(d == k)
        def _():
            fetch(k + 1)

    pltpu.make_async_copy(own[0], va.at[slot], sema.at[slot]).wait()
    for q in range(4):
        pltpu.make_async_copy(own[0].at[0], vb.at[slot, q], semb.at[slot, q]).wait()

    half = PACK // 2
    for xb in range(4):
        dx = lax.rem(x - xb + 4, 4)
        s = xb % 2
        t0[s, 0:128, :] = va[slot, dx, 0:128, 0:256]
        t0[s, 128:256, :] = va[slot, dx, 0:128, 256:512]
        t1[s, 0:half - 128, :] = va[slot, dx, 128:half, :]
        t1[s, half - 128:256, :] = vb[slot, dx, 0:384 - half, :]
        k = v.at[jnp.where(c == 0, d, dx), jnp.where(c == 0, dx, d)]
        at = 0
        for i in range(3):
            rows = min(NB, REST - i * NB)
            for j in range(i + 1):
                K[s, i * NB:i * NB + rows, j * NB:(j + 1) * NB] = k[at:at + rows, :]
                at += rows
        e = vb[slot, dx, 384 - half:half, :]
        kk = K[s][:, :REST]
        left = l_ref[0, xb]
        l0 = left[:, :TOP]
        u = (left[:, TOP:].astype(f32) + dot(l0, e, 1, 1)).astype(bf16)
        y0 = dot(l0[:, :256], t0[s], 1, 1).astype(bf16)
        y1 = dot(l0, t1[s], 1, 1).astype(bf16)
        g = dot(dot(u, kk, 1, 1).astype(bf16), kk, 1, 0).astype(bf16)
        r = dot(y1, t1[s], 1, 0) + dot(g, e, 1, 0)
        o_ref[:, xb * BG:xb * BG + 256] = (r[:, :256] + dot(y0, t0[s], 1, 0)).astype(bf16)
        o_ref[:, xb * BG + 256:xb * BG + TOP] = r[:, 256:].astype(bf16)
        o_ref[:, xb * BG + TOP:(xb + 1) * BG] = g


def apply(at, left, own, part, two):
    any_space = pl.BlockSpec(memory_space=pl.ANY)
    return pl.pallas_call(
        apply_kernel,
        out_shape=jax.ShapeDtypeStruct((BA, 16 * BG), bf16),
        grid_spec=pltpu.PrefetchScalarGridSpec(
            num_scalar_prefetch=1,
            grid=(4,),
            in_specs=[pl.BlockSpec((1, 4, BA, BG), lambda d, s: (d, 0, 0, 0))]
            + [any_space] * 8
            + [pl.BlockSpec((4, LAST, NB), lambda d, s: (0, 0, 0))] * 4,
            out_specs=pl.BlockSpec((BA, 4 * BG), lambda d, s: (0, lax.rem(s[1] - d + 4, 4))),
            scratch_shapes=[
                pltpu.VMEM((2, 4, PACK // 2, TOP), bf16),
                pltpu.VMEM((2, 4, PACK // 2, TOP), bf16),
                pltpu.VMEM((4, 4, LAST, NB), bf16),
                pltpu.VMEM((2, 256, 256), bf16),
                pltpu.VMEM((2, 256, TOP), bf16),
                pltpu.VMEM((2, REST, AP), bf16),
                pltpu.SemaphoreType.DMA((2,)),
                pltpu.SemaphoreType.DMA((2, 4)),
            ],
        ),
        compiler_params=VMEM,
        cost_estimate=cost(25),
    )(at, left, *own, *part, *two)


def tie(*arrays):
    return lax.optimization_barrier(arrays)


def shards(layer_inputs, output_grads, weight_grad):
    x, y, zh, zl, c = (lax.axis_index(n) for n in ("x", "y", "zh", "zl", "c"))
    zc = jnp.stack([2 * zh + zl, c]).astype(jnp.int32)
    at = jnp.stack([x, y, zh, c]).astype(jnp.int32)

    t = turn(output_grads, BG, lambda b: 4 * (b % 4) + b // 4, 5)
    t, weight_grad, layer_inputs = tie(t, weight_grad, layer_inputs)
    t = lax.all_to_all(t, ("x", "y"), 0, 0, tiled=True)
    w = weight_grad.reshape(BA, 2, BG).transpose(1, 0, 2)
    w_far = swap_zh(w)
    u = turn(layer_inputs, BA, lambda b: b, 2)
    w = jnp.concatenate([w, w_far], axis=0)
    t, w, u = tie(t, w, u)
    w1, w3 = along_y(w, 1), along_y(w, 3)
    mine, other = gram(zc, t)
    mine, other, u = tie(mine, other, u)
    u = lax.all_to_all(u, ("x", "y"), 0, 0, tiled=True)
    own, part = sum_over_copies(mine, other)
    m, t1 = first_inverse(zc, own, part)
    m, t1, w1, w3, u = tie(m, t1, w1, w3, u)
    w2 = [along_y(w1[:2], 1), along_y(w3[2:], 3)]
    q1 = near(t1)
    a = small_gram(u)
    m, q1, a, *w2 = tie(m, q1, a, *w2)
    one = far(q1)
    q1_other = swap_core(q1)
    t2 = second_inverse(m)
    t2, a, q1_other, one[1], one[3] = tie(t2, a, q1_other, one[1], one[3])
    q2 = near(t2)
    a = small_sum(a, c)
    act = small_inverse(a)
    act, q2, one[2] = tie(act, q2, one[2])
    two = far(q2)
    act = move(act, ("zl", "c", "y"), lambda zl, c, y: (y >> 1, y & 1, 2 * zl + c))
    left = left_rows(at, act, [w, w1, *w2, w3])
    one_other = [q1_other] + [swap_core(v) for v in one[1:]]
    return apply(at, left, one, one_other, two)


def solution(mesh):
    fine = Mesh(np.asarray(mesh.devices).reshape(tuple(SIZES.values())), tuple(SIZES))
    dp, owner = ("x", "zl", "c"), ("y", "zh")
    return jax.shard_map(
        shards,
        mesh=fine,
        in_specs=(P(dp + owner, None), P(dp + owner, None), P(dp, owner)),
        out_specs=P(dp, None),
        check_vma=False,
    )
```
